256 devices in a mesh: gx: 4 (over x), gy: 8 (over y, core), gz: 8 (over z).
Axes of the slice: x: 4, y: 4, z: 8, core: 2. Of those that a mesh axis runs over, the one named last changes fastest.
Arguments:
- orbitals: bfloat16 [32, 64, 128, 256], P('gx', 'gy', 'gz'), may hold values from -120 to 120
- cell_block: bfloat16 [729, 729], replicated, may hold values from -0.4 to 2.4, as said below
- potential: float32 [32, 64, 128], P('gx', 'gy', 'gz'), may hold values from -1 to 1
Outputs:
- orthonormal: bfloat16 [32, 64, 128, 256], P('gx', 'gy', 'gz')
The draws below stay inside these ranges and needn't reach their ends.
Inputs may be any that keep to these rules, and one draw needn't show every extreme that they name: `cell_block`: symmetric.
All inputs are finite; a program needn't handle non-finite values.
Results may differ from the reference program's by a relative error of at most 0.01.
Values may be sent and summed in bfloat16 or wider, within the bound.
A program may use at most 64 MiB of HBM per device.

```python
import math
import jax
import jax.numpy as jnp
from jax import lax

POLY = 8
BLOCK = 729
ORB = 256
NX = 32
NY = 64
NZ = 128
NODES = 262144


def draw_orbitals(key, part):
    keys = jax.random.split(jax.random.fold_in(key, 11), 3)
    row_scale = 10.0 ** jax.random.uniform(keys[0], (NX, NY, NZ, 1), jnp.float32, 0.0, 1.0)
    column_scale = 10.0 ** jax.random.uniform(keys[1], (ORB,), jnp.float32, 0.0, 1.0)
    ramp = (3.0 ** (jnp.arange(NX, dtype=jnp.float32) / NX))[:, None, None, None]
    base = jnp.clip(jax.random.normal(keys[2], (NX, NY, NZ, ORB), jnp.float32), -4.0, 4.0)
    return (base * row_scale * column_scale * ramp / 10.0).astype(jnp.bfloat16)


def draw_cell_block(key, part):
    inner_key = jax.random.fold_in(key, 23)
    entries = jnp.clip(jax.random.normal(inner_key, (BLOCK, BLOCK), jnp.float32), -4.0, 4.0)
    symmetric = (entries + entries.T) * (0.5 / math.sqrt(BLOCK))
    return (symmetric + 2.0 * jnp.eye(BLOCK, dtype=jnp.float32)).astype(jnp.bfloat16)


def steps_of(rng, shape, cuts, low, top_value):
    def one(axis_at, shards_of):
        heights = jax.random.uniform(jax.random.fold_in(jax.random.fold_in(rng, 6), axis_at), (shards_of,), jnp.float32, low / len(cuts), top_value / len(cuts))
        return jnp.repeat(jnp.exp(heights), shape[axis_at] // shards_of).reshape((-1,) + (1,) * (len(shape) - axis_at - 1))

    factor_of = one(*cuts[0])
    for cut in cuts[1:]:
        factor_of = factor_of * one(*cut)
    return factor_of


def setup_inputs(seed: int = 0) -> dict:
    arg_keys = jax.random.split(jax.random.key(seed), 4)
    orbitals = draw_orbitals(jax.random.fold_in(arg_keys[3], 71), 0)
    cell_block = draw_cell_block(jax.random.fold_in(arg_keys[3], 71), 0)
    potential = jnp.clip(jax.random.uniform(arg_keys[2], (NX, NY, NZ), jnp.float32, -1.0, 1.0) * steps_of(arg_keys[2], (NX, NY, NZ), ((0, 4), (1, 8), (2, 8)), -0.4, 0.0), -1.0, 1.0)
    return dict(orbitals=orbitals, cell_block=cell_block, potential=potential)


CENTER = 6.0
HALF_WIDTH = 8.0

def windows(values, which_axis, cell_count):
    span = POLY * cell_count
    leading = lax.slice_in_dim(values, 0, span, axis=which_axis)
    dims_now = leading.shape
    leading = leading.reshape(dims_now[:which_axis] + (cell_count, POLY) + dims_now[which_axis + 1:])
    end_nodes = lax.slice_in_dim(values, POLY, span + 1, stride=POLY, axis=which_axis)
    end_nodes = jnp.expand_dims(end_nodes, which_axis + 1)
    return jnp.concatenate([leading, end_nodes], axis=which_axis + 1)

def fold(pieces, which_axis):
    cell_count = pieces.shape[which_axis]
    first_node = lax.slice_in_dim(pieces, 0, 1, axis=which_axis + 1)
    inner_nodes = lax.slice_in_dim(pieces, 1, POLY, axis=which_axis + 1)
    last_node = lax.slice_in_dim(pieces, POLY, POLY + 1, axis=which_axis + 1)
    earlier = lax.slice_in_dim(last_node, 0, cell_count - 1, axis=which_axis)
    blank = jnp.zeros_like(lax.slice_in_dim(last_node, 0, 1, axis=which_axis))
    first_node = first_node + jnp.concatenate([blank, earlier], axis=which_axis)
    merged = jnp.concatenate([first_node, inner_nodes], axis=which_axis + 1)
    dims_now = merged.shape
    merged = merged.reshape(dims_now[:which_axis] + (cell_count * POLY,) + dims_now[which_axis + 2:])
    closing = lax.slice_in_dim(last_node, cell_count - 1, cell_count, axis=which_axis)
    closing = jnp.squeeze(closing, which_axis + 1)
    return jnp.concatenate([merged, closing], axis=which_axis)

def cell_product(extended, cell_block):
    side = POLY + 1
    count_x = (extended.shape[0] - 1) // POLY
    count_y = (extended.shape[1] - 1) // POLY
    count_z = (extended.shape[2] - 1) // POLY
    pieces = windows(extended, 0, count_x)
    pieces = windows(pieces, 2, count_y)
    pieces = windows(pieces, 4, count_z)
    width = pieces.shape[-1]
    cells = pieces.transpose(0, 2, 4, 1, 3, 5, 6).reshape(count_x * count_y * count_z, side ** 3, width)
    product = jnp.einsum('ij,cjo->cio', cell_block.astype(jnp.float32), cells.astype(jnp.float32))
    product = product.reshape(count_x, count_y, count_z, side, side, side, width).transpose(0, 3, 1, 4, 2, 5, 6)
    return fold(fold(fold(product, 4), 2), 0)

def wrap_extend(values):
    values = jnp.concatenate([values, values[:1]], axis=0)
    values = jnp.concatenate([values, values[:, :1]], axis=1)
    return jnp.concatenate([values, values[:, :, :1]], axis=2)

def apply_operator(values, cell_block, potential):
    extended = wrap_extend(values)
    slab_count = NX // POLY

    def one_slab(slab_number):
        start = slab_number * POLY
        slab = lax.dynamic_slice_in_dim(extended, start, POLY + 1, 0)
        slab_sum = cell_product(slab, cell_block)
        slab_sum = jnp.concatenate([slab_sum[:, :1] + slab_sum[:, NY:], slab_sum[:, 1:NY]], axis=1)
        return jnp.concatenate([slab_sum[:, :, :1] + slab_sum[:, :, NZ:], slab_sum[:, :, 1:NZ]], axis=2)
    stacked = lax.map(one_slab, jnp.arange(slab_count, dtype=jnp.int32))
    carried = jnp.roll(stacked[:, POLY], 1, axis=0)
    leading = stacked[:, :1] + carried[:, None]
    assembled = jnp.concatenate([leading, stacked[:, 1:POLY]], axis=1).reshape(NX, NY, NZ, ORB)
    return assembled + potential[..., None] * values.astype(jnp.float32)

def reference(orbitals, cell_block, potential):
    start_values = orbitals.astype(jnp.float32)
    image = apply_operator(orbitals, cell_block, potential)
    first = ((image - CENTER * start_values) / HALF_WIDTH).astype(jnp.bfloat16)
    image = apply_operator(first, cell_block, potential)
    second = (2.0 * (image - CENTER * first.astype(jnp.float32)) / HALF_WIDTH - start_values).astype(jnp.bfloat16)
    image = apply_operator(second, cell_block, potential)
    filtered = (2.0 * (image - CENTER * second.astype(jnp.float32)) / HALF_WIDTH - first.astype(jnp.float32)).astype(jnp.bfloat16)
    slab_rows = filtered.reshape(NX // POLY, -1, ORB)

    def slab_gram(row_block):
        floats = row_block.astype(jnp.float32)
        return jnp.dot(floats.T, floats, precision=lax.Precision.HIGHEST)
    gram = jnp.sum(lax.map(slab_gram, slab_rows), axis=0) / NODES
    lower = jnp.linalg.cholesky(gram)
    inverse = jax.scipy.linalg.solve_triangular(lower, jnp.eye(ORB, dtype=jnp.float32), lower=True)
    right_factor = inverse.T

    def slab_rotate(row_block):
        return jnp.dot(row_block.astype(jnp.float32), right_factor, precision=lax.Precision.HIGHEST).astype(jnp.bfloat16)
    return lax.map(slab_rotate, slab_rows).reshape(NX, NY, NZ, ORB)
```

```python
import functools

import jax
import jax.numpy as jnp
import ml_dtypes
import numpy as np
from jax import lax
from jax.experimental import pallas as pl
from jax.experimental.pallas import tpu as pltpu
from jax.sharding import PartitionSpec as P

POLY = 8
SIDE = POLY + 1
CENTER = 6.0
HALF_WIDTH = 8.0
MESH = pl.DeviceIdType.MESH
F32 = jnp.float32
BF16 = jnp.bfloat16

COLS = SIDE * SIDE * POLY
ROWS = 736
PLANE = ROWS - COLS
LINE = SIDE * POLY

DIRECTIONS = [
    (dx, dy, dz)
    for dx, dy, dz in [
        (-1, 0, 0), (1, 0, 0), (0, -1, 0), (0, 1, 0), (0, 0, -1), (0, 0, 1),
    ]
] + [
    (dx, dy, dz)
    for dx in (-1, 0, 1)
    for dy in (-1, 0, 1)
    for dz in (-1, 0, 1)
    if abs(dx) + abs(dy) + abs(dz) >= 2
]
LOW = [d for d in DIRECTIONS if max(d) <= 0]
HIGH = [d for d in DIRECTIONS if min(d) >= 0]


def column_rows(d):
    if d[2] != 0:
        return 0
    return 2 * LINE if 0 in d[:2] else 2 * POLY


def plane_rows(d):
    return 96 if d[:2] == (0, 0) else 16


OFFSET = {}
_at = 0
for _d in DIRECTIONS:
    OFFSET[_d] = _at
    _at += column_rows(_d) + plane_rows(_d)
MESSAGE_ROWS = _at


def message_rows(dirs):
    return sum(column_rows(d) + plane_rows(d) for d in dirs)


TOP = [d for d in DIRECTIONS if d[2] <= 0]
BOTTOM = [d for d in DIRECTIONS if d[2] > 0]


def edge_nodes(step):
    return [8] if step > 0 else [0] if step < 0 else list(range(SIDE))


def plane_nodes(d):
    return [(i, j) for i in edge_nodes(d[0]) for j in edge_nodes(d[1])]


def tables():
    order = np.zeros((ROWS, SIDE**3), np.float32)
    for i in range(SIDE):
        for j in range(SIDE):
            for k in range(POLY):
                order[i * LINE + j * POLY + k, i * 81 + j * 9 + k] = 1
            order[COLS + i * 9 + j, i * 81 + j * 9 + POLY] = 1
    pick = np.zeros((sum(plane_rows(d) for d in DIRECTIONS), ROWS), np.float32)
    at = 0
    for d in DIRECTIONS:
        for t, (i, j) in enumerate(plane_nodes(d)):
            pick[at + t, i * LINE + j * POLY if d[2] < 0 else COLS + i * 9 + j] = 1
        at += plane_rows(d)
    top = np.zeros((PLANE, sum(plane_rows(d) for d in TOP)), np.float32)
    at = 0
    for d in TOP:
        for t, (i, j) in enumerate(plane_nodes((-d[0], -d[1], 0))):
            top[i * 9 + j, at + t] = 1
        at += plane_rows(d)
    bottom = np.zeros((COLS, sum(plane_rows(d) for d in BOTTOM)), np.float32)
    at = 0
    for d in BOTTOM:
        for t, (i, j) in enumerate(plane_nodes((-d[0], -d[1], 0))):
            bottom[i * LINE + j * POLY, at + t] = 1
        at += plane_rows(d)
    insert = np.zeros((COLS, PLANE), np.float32)
    for i in range(SIDE):
        for j in range(SIDE):
            insert[i * LINE + j * POLY, i * 9 + j] = 1
    made = [order, pick, top, bottom, np.concatenate([insert, insert], 1), insert.T]
    return [m.astype(ml_dtypes.bfloat16) for m in made]


def dot(a, b):
    return jnp.dot(a, b, preferred_element_type=F32)


def filter_kernel(
    sizes,
    orbitals, cell, potential, order, pick, top, bottom, insert, extract,
    filtered, gram,
    operator, shift, sums, field0, field1, field2, send, recv, total, parts, planes, whole,
    send_sem, recv_sem, part_send_sem, part_recv_sem,
):
    nx, ny, nz = sizes
    me = (lax.axis_index("gx"), lax.axis_index("gy"), lax.axis_index("gz"))
    group = nx * ny
    mine = me[0] * ny + me[1]
    chunk = total.shape[0] // group

    def towards(d):
        return tuple(
            m if s == 0 else lax.rem(m + (s + n), n) for m, s, n in zip(me, d, sizes)
        )

    def member(t):
        other = lax.rem(mine + t, group)
        return other, (other // ny, lax.rem(other, ny), me[2])

    def above(t):
        return me[0], me[1], lax.rem(me[2] + t, nz)

    def tile(n):
        return pl.ds(pl.multiple_of(n * chunk, chunk), chunk)

    barrier = pltpu.get_barrier_semaphore()
    for d in DIRECTIONS:
        pl.semaphore_signal(barrier, inc=1, device_id=towards(d), device_id_type=MESH)

    @pl.loop(1, group)
    def _(t):
        pl.semaphore_signal(barrier, inc=1, device_id=member(t)[1], device_id_type=MESH)

    @pl.loop(1, nz)
    def _(t):
        pl.semaphore_signal(barrier, inc=1, device_id=above(t), device_id_type=MESH)

    def column_slices(d):
        for c in range(2):
            if d[1] == 0:
                yield c, (0 if d[0] < 0 else 8) * LINE, LINE
            else:
                for i in edge_nodes(d[0]):
                    yield c, i * LINE + (0 if d[1] < 0 else 8) * POLY, POLY

    def pack(number, dirs):
        source = jnp.concatenate([sums[0, :COLS], sums[1, COLS:]], axis=0).astype(BF16)
        small = dot(pick[...], source).astype(BF16)
        at = 0
        for d in DIRECTIONS:
            columns, width = column_rows(d), plane_rows(d)
            if d in dirs:
                if columns:
                    pieces = [sums[c, r : r + w] for c, r, w in column_slices(d)]
                    send[number, pl.ds(OFFSET[d], columns)] = jnp.concatenate(
                        pieces, axis=0
                    ).astype(BF16)
                send[number, pl.ds(OFFSET[d] + columns, width)] = small[at : at + width]
            at += width

    def copies(number, dirs):
        for d in dirs:
            rows = pl.ds(OFFSET[d], column_rows(d) + plane_rows(d))
            yield pltpu.make_async_remote_copy(
                src_ref=send.at[number, rows],
                dst_ref=recv.at[number, rows],
                send_sem=send_sem.at[number],
                recv_sem=recv_sem.at[number],
                device_id=towards(d),
                device_id_type=MESH,
            )

    def finish(number, dirs, semaphore):
        arrived = recv.at[number, pl.ds(0, message_rows(dirs))]
        pltpu.make_async_copy(arrived, arrived, semaphore.at[number]).wait()

    def unpack(number, dirs):
        for d in dirs:
            if column_rows(d):
                got = recv[number, pl.ds(OFFSET[d], column_rows(d))].astype(F32)
                at = 0
                for c, r, w in column_slices((-d[0], -d[1], 0)):
                    sums[c, r : r + w] += got[at : at + w]
                    at += w

        def plane_parts(wanted):
            return jnp.concatenate(
                [
                    recv[number, pl.ds(OFFSET[d] + column_rows(d), plane_rows(d))]
                    if d in dirs
                    else jnp.zeros((plane_rows(d), recv.shape[-1]), BF16)
                    for d in wanted
                ],
                axis=0,
            )

        if dirs is not HIGH:
            sums[1, COLS:] += dot(top[...], plane_parts(TOP))
        if dirs is not LOW:
            sums[0, :COLS] += dot(bottom[...], plane_parts(BOTTOM))

    def exchange(number, dirs, meanwhile=None):
        pack(number, dirs)
        for copy in copies(number, dirs):
            copy.start()
        if meanwhile is not None:
            meanwhile()
        finish(number, dirs, recv_sem)
        unpack(number, dirs)

    def hold(field, first, second, last):
        closing = dot(extract[...], second.astype(BF16))
        field[0] = jnp.concatenate([first, closing], axis=0).astype(BF16)
        field[1] = jnp.concatenate([second, last], axis=0).astype(BF16)

    def apply_operator(field):
        for c in range(2):
            values = field[c]
            image = dot(operator[...], values)
            sums[c, :COLS] = image[:COLS] + shift[c] * values.astype(F32)[:COLS]
            sums[c, COLS:] = image[COLS:]
        plane = sums[0, COLS:]
        high = plane.astype(BF16).astype(F32)
        split = jnp.concatenate([high, plane - high], axis=0).astype(BF16)
        sums[1, :COLS] += dot(insert[...], split)

    sums[...] = jnp.zeros_like(sums)
    shift[...] = jnp.zeros_like(shift)
    for i in range(POLY):
        layer = orbitals[i].astype(F32).reshape(POLY, 2, POLY, -1)
        scale = jnp.broadcast_to(
            (potential[i] - CENTER)[:, :, None], (POLY, 2 * POLY, layer.shape[-1])
        ).reshape(layer.shape)
        for c in range(2):
            sums[c, i * LINE : i * LINE + 64] = layer[:, c].reshape(64, -1)
            shift[c, i * LINE : i * LINE + 64] = scale[:, c].reshape(64, -1)

    def make_operator():
        turned = dot(order[...], cell[...]).astype(BF16)
        operator[...] = lax.dot_general(
            turned, order[...], (((1,), (1,)), ((), ())), preferred_element_type=F32
        ).astype(BF16)

    pl.semaphore_wait(barrier, len(DIRECTIONS) + group - 1 + nz - 1)
    exchange(0, LOW, make_operator)
    hold(field0, sums[0, :COLS], sums[1, :COLS], sums[1, COLS:])

    apply_operator(field0)
    exchange(1, DIRECTIONS)
    scaled = [sums[c] / HALF_WIDTH for c in range(2)]
    hold(field1, scaled[0][:COLS], scaled[1][:COLS], scaled[1][COLS:])

    apply_operator(field1)
    exchange(2, DIRECTIONS)
    scaled = [2.0 * sums[c] / HALF_WIDTH - field0[c].astype(F32) for c in range(2)]
    hold(field2, scaled[0][:COLS], scaled[1][:COLS], scaled[1][COLS:])

    apply_operator(field2)
    exchange(3, HIGH)
    for i in range(POLY):
        rows = slice(i * LINE, i * LINE + 64)
        halves = []
        for c in range(2):
            before = field1[c].astype(F32)[rows]
            now = 2.0 * sums[c, rows] / HALF_WIDTH - before
            halves.append(now.reshape(POLY, 1, POLY, -1))
        layer = jnp.concatenate(halves, axis=1).reshape(POLY, 2 * POLY, -1)
        filtered[i] = layer.astype(BF16)

    flat = filtered[...].reshape(-1, filtered.shape[-1])
    total[...] = lax.dot_general(
        flat, flat, (((0,), (0,)), ((), ())), preferred_element_type=F32
    )

    def part_copy(phase, source, target, device):
        return pltpu.make_async_remote_copy(
            src_ref=source,
            dst_ref=target,
            send_sem=part_send_sem.at[phase],
            recv_sem=part_recv_sem.at[phase],
            device_id=device,
            device_id_type=MESH,
        )

    def part_wait(buffer, count, semaphore):
        some = buffer.at[pl.ds(0, count)]
        pltpu.make_async_copy(some, some, semaphore).wait()

    @pl.loop(1, group)
    def _(t):
        other, device = member(t)
        part_copy(0, total.at[tile(other)], parts.at[mine], device).start()

    parts[mine] = total[tile(mine)]
    part_wait(parts, group - 1, part_recv_sem.at[0])
    planes[me[2]] = jnp.sum(parts[...], axis=0)

    @pl.loop(1, nz)
    def _(t):
        part_copy(1, planes.at[me[2]], planes.at[me[2]], above(t)).start()

    part_wait(planes, nz - 1, part_recv_sem.at[1])
    whole[tile(mine)] = jnp.sum(planes[...], axis=0)

    @pl.loop(1, group)
    def _(t):
        part_copy(2, whole.at[tile(mine)], whole.at[tile(mine)], member(t)[1]).start()

    part_wait(whole, (group - 1) * chunk, part_recv_sem.at[2])
    gram[...] = whole[...]

    for number, dirs in enumerate((LOW, DIRECTIONS, DIRECTIONS, HIGH)):
        finish(number, dirs, send_sem)
    part_wait(parts, group - 1, part_send_sem.at[0])
    part_wait(planes, nz - 1, part_send_sem.at[1])
    part_wait(whole, (group - 1) * chunk, part_send_sem.at[2])


def filter_and_gram(sizes, orbitals, cell_block, potential):
    width = orbitals.shape[-1]
    group = sizes[0] * sizes[1]
    made = tables()
    vmem = pl.BlockSpec(memory_space=pltpu.VMEM)
    return pl.pallas_call(
        functools.partial(filter_kernel, sizes),
        out_shape=[
            jax.ShapeDtypeStruct(orbitals.shape, BF16),
            jax.ShapeDtypeStruct((width, width), F32),
        ],
        in_specs=[vmem] * (3 + len(made)),
        out_specs=[vmem] * 2,
        scratch_shapes=[
            pltpu.VMEM((ROWS, ROWS), BF16),
            pltpu.VMEM((2, COLS, width), F32),
            pltpu.VMEM((2, ROWS, width), F32),
            pltpu.VMEM((2, ROWS, width), BF16),
            pltpu.VMEM((2, ROWS, width), BF16),
            pltpu.VMEM((2, ROWS, width), BF16),
            pltpu.VMEM((4, MESSAGE_ROWS, width), BF16),
            pltpu.VMEM((4, MESSAGE_ROWS, width), BF16),
            pltpu.VMEM((width, width), F32),
            pltpu.VMEM((group, width // group, width), F32),
            pltpu.VMEM((sizes[2], width // group, width), F32),
            pltpu.VMEM((width, width), F32),
            pltpu.SemaphoreType.DMA((4,)),
            pltpu.SemaphoreType.DMA((4,)),
            pltpu.SemaphoreType.DMA((3,)),
            pltpu.SemaphoreType.DMA((3,)),
        ],
        compiler_params=pltpu.CompilerParams(
            collective_id=0, has_side_effects=True, vmem_limit_bytes=48 * 2**20
        ),
    )(orbitals, cell_block, potential, *made)


def local(sizes, orbitals, cell_block, potential):
    filtered, gram = filter_and_gram(sizes, orbitals, cell_block, potential)
    width = filtered.shape[-1]
    flat_rows = filtered.reshape(-1, width)
    node_total = flat_rows.shape[0] * sizes[0] * sizes[1] * sizes[2]
    lower = jnp.linalg.cholesky(gram / node_total)
    inverse = jax.scipy.linalg.solve_triangular(
        lower, jnp.eye(width, dtype=F32), lower=True
    )
    right_factor = inverse.T
    factor_high = right_factor.astype(BF16)
    factor_low = (right_factor - factor_high.astype(F32)).astype(BF16)
    rotated = dot(flat_rows, factor_high) + dot(flat_rows, factor_low)
    return rotated.astype(BF16).reshape(filtered.shape)


def solution(mesh):
    sizes = tuple(mesh.shape[name] for name in ("gx", "gy", "gz"))
    placed = (P("gx", "gy", "gz", None), P(), P("gx", "gy", "gz"))
    return jax.shard_map(
        functools.partial(local, sizes),
        mesh=mesh,
        in_specs=placed,
        out_specs=P("gx", "gy", "gz", None),
        check_vma=False,
    )
```

```python
import functools

import jax
import jax.numpy as jnp
import ml_dtypes
import numpy as np
from jax import lax
from jax.experimental import pallas as pl
from jax.experimental.pallas import tpu as pltpu
from jax.sharding import PartitionSpec as P

POLY = 8
SIDE = POLY + 1
CENTER = 6.0
HALF_WIDTH = 8.0
MESH = pl.DeviceIdType.MESH
F32 = jnp.float32
BF16 = jnp.bfloat16
HIGHEST = lax.Precision.HIGHEST
TILE = 8

COLS = SIDE * SIDE * POLY
ROWS = 736
PLANE = ROWS - COLS
LINE = SIDE * POLY

DIRECTIONS = [
    (dx, dy, dz)
    for dx, dy, dz in [
        (-1, 0, 0), (1, 0, 0), (0, -1, 0), (0, 1, 0), (0, 0, -1), (0, 0, 1),
    ]
] + [
    (dx, dy, dz)
    for dx in (-1, 0, 1)
    for dy in (-1, 0, 1)
    for dz in (-1, 0, 1)
    if abs(dx) + abs(dy) + abs(dz) >= 2
]
LOW = [d for d in DIRECTIONS if max(d) <= 0]
HIGH = [d for d in DIRECTIONS if min(d) >= 0]


def column_rows(d):
    if d[2] != 0:
        return 0
    return 2 * LINE if 0 in d[:2] else 2 * POLY


def plane_rows(d):
    return 96 if d[:2] == (0, 0) else 16


OFFSET = {}
_at = 0
for _d in DIRECTIONS:
    OFFSET[_d] = _at
    _at += column_rows(_d) + plane_rows(_d)
MESSAGE_ROWS = _at


def message_rows(dirs):
    return sum(column_rows(d) + plane_rows(d) for d in dirs)


TOP = [d for d in DIRECTIONS if d[2] <= 0]
BOTTOM = [d for d in DIRECTIONS if d[2] > 0]


def edge_nodes(step):
    return [8] if step > 0 else [0] if step < 0 else list(range(SIDE))


def plane_nodes(d):
    return [(i, j) for i in edge_nodes(d[0]) for j in edge_nodes(d[1])]


def tables():
    order = np.zeros((ROWS, SIDE**3), np.float32)
    for i in range(SIDE):
        for j in range(SIDE):
            for k in range(POLY):
                order[i * LINE + j * POLY + k, i * 81 + j * 9 + k] = 1
            order[COLS + i * 9 + j, i * 81 + j * 9 + POLY] = 1
    pick = np.zeros((sum(plane_rows(d) for d in DIRECTIONS), ROWS), np.float32)
    at = 0
    for d in DIRECTIONS:
        for t, (i, j) in enumerate(plane_nodes(d)):
            pick[at + t, i * LINE + j * POLY if d[2] < 0 else COLS + i * 9 + j] = 1
        at += plane_rows(d)
    top = np.zeros((PLANE, sum(plane_rows(d) for d in TOP)), np.float32)
    at = 0
    for d in TOP:
        for t, (i, j) in enumerate(plane_nodes((-d[0], -d[1], 0))):
            top[i * 9 + j, at + t] = 1
        at += plane_rows(d)
    bottom = np.zeros((COLS, sum(plane_rows(d) for d in BOTTOM)), np.float32)
    at = 0
    for d in BOTTOM:
        for t, (i, j) in enumerate(plane_nodes((-d[0], -d[1], 0))):
            bottom[i * LINE + j * POLY, at + t] = 1
        at += plane_rows(d)
    insert = np.zeros((COLS, PLANE), np.float32)
    for i in range(SIDE):
        for j in range(SIDE):
            insert[i * LINE + j * POLY, i * 9 + j] = 1
    made = [order, pick, top, bottom, np.concatenate([insert, insert], 1), insert.T]
    return [m.astype(ml_dtypes.bfloat16) for m in made]


def dot(a, b):
    return jnp.dot(a, b, preferred_element_type=F32)


def filter_kernel(
    sizes,
    orbitals, cell, potential, order, pick, top, bottom, insert, extract,
    filtered, gram,
    operator, shift, sums, field0, field1, field2, send, recv, total, parts, planes, whole,
    send_sem, recv_sem, part_send_sem, part_recv_sem,
):
    nx, ny, nz = sizes
    me = (lax.axis_index("gx"), lax.axis_index("gy"), lax.axis_index("gz"))
    group = nx * ny
    mine = me[0] * ny + me[1]
    chunk = total.shape[0] // group

    def towards(d):
        return tuple(
            m if s == 0 else lax.rem(m + (s + n), n) for m, s, n in zip(me, d, sizes)
        )

    def member(t):
        other = lax.rem(mine + t, group)
        return other, (other // ny, lax.rem(other, ny), me[2])

    def above(t):
        return me[0], me[1], lax.rem(me[2] + t, nz)

    def tile(n):
        return pl.ds(pl.multiple_of(n * chunk, chunk), chunk)

    barrier = pltpu.get_barrier_semaphore()
    for d in DIRECTIONS:
        pl.semaphore_signal(barrier, inc=1, device_id=towards(d), device_id_type=MESH)

    @pl.loop(1, group)
    def _(t):
        pl.semaphore_signal(barrier, inc=1, device_id=member(t)[1], device_id_type=MESH)

    @pl.loop(1, nz)
    def _(t):
        pl.semaphore_signal(barrier, inc=1, device_id=above(t), device_id_type=MESH)

    def column_slices(d):
        for c in range(2):
            if d[1] == 0:
                yield c, (0 if d[0] < 0 else 8) * LINE, LINE
            else:
                for i in edge_nodes(d[0]):
                    yield c, i * LINE + (0 if d[1] < 0 else 8) * POLY, POLY

    def pack(number, dirs):
        source = jnp.concatenate([sums[0, :COLS], sums[1, COLS:]], axis=0).astype(BF16)
        small = dot(pick[...], source).astype(BF16)
        at = 0
        for d in DIRECTIONS:
            columns, width = column_rows(d), plane_rows(d)
            if d in dirs:
                if columns:
                    pieces = [sums[c, r : r + w] for c, r, w in column_slices(d)]
                    send[number, pl.ds(OFFSET[d], columns)] = jnp.concatenate(
                        pieces, axis=0
                    ).astype(BF16)
                send[number, pl.ds(OFFSET[d] + columns, width)] = small[at : at + width]
            at += width

    def copies(number, dirs):
        for d in dirs:
            rows = pl.ds(OFFSET[d], column_rows(d) + plane_rows(d))
            yield pltpu.make_async_remote_copy(
                src_ref=send.at[number, rows],
                dst_ref=recv.at[number, rows],
                send_sem=send_sem.at[number],
                recv_sem=recv_sem.at[number],
                device_id=towards(d),
                device_id_type=MESH,
            )

    def finish(number, dirs, semaphore):
        arrived = recv.at[number, pl.ds(0, message_rows(dirs))]
        pltpu.make_async_copy(arrived, arrived, semaphore.at[number]).wait()

    def unpack(number, dirs):
        for d in dirs:
            if column_rows(d):
                got = recv[number, pl.ds(OFFSET[d], column_rows(d))].astype(F32)
                at = 0
                for c, r, w in column_slices((-d[0], -d[1], 0)):
                    sums[c, r : r + w] += got[at : at + w]
                    at += w

        def plane_parts(wanted):
            return jnp.concatenate(
                [
                    recv[number, pl.ds(OFFSET[d] + column_rows(d), plane_rows(d))]
                    if d in dirs
                    else jnp.zeros((plane_rows(d), recv.shape[-1]), BF16)
                    for d in wanted
                ],
                axis=0,
            )

        if dirs is not HIGH:
            sums[1, COLS:] += dot(top[...], plane_parts(TOP))
        if dirs is not LOW:
            sums[0, :COLS] += dot(bottom[...], plane_parts(BOTTOM))

    def exchange(number, dirs, meanwhile=None):
        pack(number, dirs)
        for copy in copies(number, dirs):
            copy.start()
        if meanwhile is not None:
            meanwhile()
        finish(number, dirs, recv_sem)
        unpack(number, dirs)

    def hold(field, first, second, last):
        closing = dot(extract[...], second.astype(BF16))
        field[0] = jnp.concatenate([first, closing], axis=0).astype(BF16)
        field[1] = jnp.concatenate([second, last], axis=0).astype(BF16)

    def apply_operator(field):
        for c in range(2):
            values = field[c]
            image = dot(operator[...], values)
            sums[c, :COLS] = image[:COLS] + shift[c] * values.astype(F32)[:COLS]
            sums[c, COLS:] = image[COLS:]
        plane = sums[0, COLS:]
        high = plane.astype(BF16).astype(F32)
        split = jnp.concatenate([high, plane - high], axis=0).astype(BF16)
        sums[1, :COLS] += dot(insert[...], split)

    sums[...] = jnp.zeros_like(sums)
    shift[...] = jnp.zeros_like(shift)
    for i in range(POLY):
        layer = orbitals[i].astype(F32).reshape(POLY, 2, POLY, -1)
        scale = jnp.broadcast_to(
            (potential[i] - CENTER)[:, :, None], (POLY, 2 * POLY, layer.shape[-1])
        ).reshape(layer.shape)
        for c in range(2):
            sums[c, i * LINE : i * LINE + 64] = layer[:, c].reshape(64, -1)
            shift[c, i * LINE : i * LINE + 64] = scale[:, c].reshape(64, -1)

    def make_operator():
        turned = dot(order[...], cell[...]).astype(BF16)
        operator[...] = lax.dot_general(
            turned, order[...], (((1,), (1,)), ((), ())), preferred_element_type=F32
        ).astype(BF16)

    pl.semaphore_wait(barrier, len(DIRECTIONS) + group - 1 + nz - 1)
    exchange(0, LOW, make_operator)
    hold(field0, sums[0, :COLS], sums[1, :COLS], sums[1, COLS:])

    apply_operator(field0)
    exchange(1, DIRECTIONS)
    scaled = [sums[c] / HALF_WIDTH for c in range(2)]
    hold(field1, scaled[0][:COLS], scaled[1][:COLS], scaled[1][COLS:])

    apply_operator(field1)
    exchange(2, DIRECTIONS)
    scaled = [2.0 * sums[c] / HALF_WIDTH - field0[c].astype(F32) for c in range(2)]
    hold(field2, scaled[0][:COLS], scaled[1][:COLS], scaled[1][COLS:])

    apply_operator(field2)
    exchange(3, HIGH)
    for i in range(POLY):
        rows = slice(i * LINE, i * LINE + 64)
        halves = []
        for c in range(2):
            before = field1[c].astype(F32)[rows]
            now = 2.0 * sums[c, rows] / HALF_WIDTH - before
            halves.append(now.reshape(POLY, 1, POLY, -1))
        layer = jnp.concatenate(halves, axis=1).reshape(POLY, 2 * POLY, -1)
        filtered[i] = layer.astype(BF16)

    flat = filtered[...].reshape(-1, filtered.shape[-1])
    total[...] = lax.dot_general(
        flat, flat, (((0,), (0,)), ((), ())), preferred_element_type=F32
    )

    def part_copy(phase, source, target, device):
        return pltpu.make_async_remote_copy(
            src_ref=source,
            dst_ref=target,
            send_sem=part_send_sem.at[phase],
            recv_sem=part_recv_sem.at[phase],
            device_id=device,
            device_id_type=MESH,
        )

    def part_wait(buffer, count, semaphore):
        some = buffer.at[pl.ds(0, count)]
        pltpu.make_async_copy(some, some, semaphore).wait()

    @pl.loop(1, group)
    def _(t):
        other, device = member(t)
        part_copy(0, total.at[tile(other)], parts.at[mine], device).start()

    parts[mine] = total[tile(mine)]
    part_wait(parts, group - 1, part_recv_sem.at[0])
    planes[me[2]] = jnp.sum(parts[...], axis=0)

    @pl.loop(1, nz)
    def _(t):
        part_copy(1, planes.at[me[2]], planes.at[me[2]], above(t)).start()

    part_wait(planes, nz - 1, part_recv_sem.at[1])
    whole[tile(mine)] = jnp.sum(planes[...], axis=0)

    @pl.loop(1, group)
    def _(t):
        part_copy(2, whole.at[tile(mine)], whole.at[tile(mine)], member(t)[1]).start()

    part_wait(whole, (group - 1) * chunk, part_recv_sem.at[2])
    gram[...] = whole[...]

    for number, dirs in enumerate((LOW, DIRECTIONS, DIRECTIONS, HIGH)):
        finish(number, dirs, send_sem)
    part_wait(parts, group - 1, part_send_sem.at[0])
    part_wait(planes, nz - 1, part_send_sem.at[1])
    part_wait(whole, (group - 1) * chunk, part_send_sem.at[2])


def filter_and_gram(sizes, orbitals, cell_block, potential):
    width = orbitals.shape[-1]
    group = sizes[0] * sizes[1]
    made = tables()
    vmem = pl.BlockSpec(memory_space=pltpu.VMEM)
    return pl.pallas_call(
        functools.partial(filter_kernel, sizes),
        out_shape=[
            jax.ShapeDtypeStruct(orbitals.shape, BF16),
            jax.ShapeDtypeStruct((width, width), F32),
        ],
        in_specs=[vmem] * (3 + len(made)),
        out_specs=[vmem] * 2,
        scratch_shapes=[
            pltpu.VMEM((ROWS, ROWS), BF16),
            pltpu.VMEM((2, COLS, width), F32),
            pltpu.VMEM((2, ROWS, width), F32),
            pltpu.VMEM((2, ROWS, width), BF16),
            pltpu.VMEM((2, ROWS, width), BF16),
            pltpu.VMEM((2, ROWS, width), BF16),
            pltpu.VMEM((4, MESSAGE_ROWS, width), BF16),
            pltpu.VMEM((4, MESSAGE_ROWS, width), BF16),
            pltpu.VMEM((width, width), F32),
            pltpu.VMEM((group, width // group, width), F32),
            pltpu.VMEM((sizes[2], width // group, width), F32),
            pltpu.VMEM((width, width), F32),
            pltpu.SemaphoreType.DMA((4,)),
            pltpu.SemaphoreType.DMA((4,)),
            pltpu.SemaphoreType.DMA((3,)),
            pltpu.SemaphoreType.DMA((3,)),
        ],
        compiler_params=pltpu.CompilerParams(
            collective_id=0, has_side_effects=True, vmem_limit_bytes=48 * 2**20
        ),
    )(orbitals, cell_block, potential, *made)


def spread_lane(x, n):
    return jnp.broadcast_to(x[:, n : n + 1], x.shape)


def spread_row(x, n):
    return jnp.broadcast_to(x[n : n + 1], x.shape)


def inverse_factor(rows):
    count = len(rows)
    shape = rows[0].shape
    height = lax.broadcasted_iota(jnp.int32, shape, 0)
    lane = lax.broadcasted_iota(jnp.int32, shape, 1)
    rows = list(rows)
    made = [jnp.where(lane == height + TILE * g, 1.0, 0.0).astype(F32) for g in range(count)]
    for b in range(count):
        lead, image = rows[b], made[b]
        columns = [spread_lane(lead, TILE * b + t) for t in range(TILE)]
        recips, coefs, lead_rows, image_rows = [], [], [], []
        pivots = jnp.ones(shape, F32)
        for t in range(TILE):
            pivot = spread_row(columns[t], t)
            recips.append(1.0 / pivot)
            pivots = jnp.where(height == t, pivot, pivots)
            factor = jnp.where(height > t, columns[t] * recips[t], 0.0)
            coefs.append({u: spread_row(columns[u], t) for u in range(t + 1, TILE)})
            for u in range(t + 1, TILE):
                columns[u] = columns[u] - factor * coefs[t][u]
            lead_rows.append(spread_row(lead, t))
            image_rows.append(spread_row(image, t))
            lead = lead - factor * lead_rows[t]
            image = image - factor * image_rows[t]
        made[b] = image * lax.rsqrt(pivots)
        for g in range(b + 1, count):
            entries = [spread_lane(rows[g], TILE * b + t) for t in range(TILE)]
            for t in range(TILE):
                factor = entries[t] * recips[t]
                for u in range(t + 1, TILE):
                    entries[u] = entries[u] - factor * coefs[t][u]
                rows[g] = rows[g] - factor * lead_rows[t]
                made[g] = made[g] - factor * image_rows[t]
    return jnp.concatenate(made, axis=0)


def full(a, b, contract=((1,), (0,))):
    return lax.dot_general(a, b, (contract, ((), ())), precision=HIGHEST, preferred_element_type=F32)


NT = ((1,), (1,))


def rotate_kernel(node_total, gram, filtered, out):
    half = gram.shape[0] // 2
    scaled = gram[...] / node_total

    def groups(block):
        return [block[TILE * g : TILE * (g + 1)] for g in range(half // TILE)]

    first = inverse_factor(groups(scaled[:half, :half]))
    below = full(scaled[half:, :half], first, NT)
    second = inverse_factor(groups(scaled[half:, half:] - full(below, below, NT)))
    corner = -full(second, full(below, first))
    inverse = jnp.concatenate(
        [
            jnp.concatenate([first, jnp.zeros((half, half), F32)], axis=1),
            jnp.concatenate([corner, second], axis=1),
        ],
        axis=0,
    )
    high = inverse.astype(BF16)
    low = (inverse - high.astype(F32)).astype(BF16)
    flat = filtered[...].reshape(-1, filtered.shape[-1])
    dims = (NT, ((), ()))
    rotated = lax.dot_general(flat, high, dims, preferred_element_type=F32) + lax.dot_general(
        flat, low, dims, preferred_element_type=F32
    )
    out[...] = rotated.astype(BF16).reshape(out.shape)


def rotate(node_total, gram, filtered):
    vmem = pl.BlockSpec(memory_space=pltpu.VMEM)
    return pl.pallas_call(
        functools.partial(rotate_kernel, node_total),
        out_shape=jax.ShapeDtypeStruct(filtered.shape, BF16),
        in_specs=[vmem] * 2,
        out_specs=vmem,
        compiler_params=pltpu.CompilerParams(vmem_limit_bytes=32 * 2**20),
    )(gram, filtered)


def local(sizes, orbitals, cell_block, potential):
    filtered, gram = filter_and_gram(sizes, orbitals, cell_block, potential)
    node_total = filtered.size // filtered.shape[-1] * sizes[0] * sizes[1] * sizes[2]
    return rotate(node_total, gram, filtered)


def solution(mesh):
    sizes = tuple(mesh.shape[name] for name in ("gx", "gy", "gz"))
    placed = (P("gx", "gy", "gz", None), P(), P("gx", "gy", "gz"))
    return jax.shard_map(
        functools.partial(local, sizes),
        mesh=mesh,
        in_specs=placed,
        out_specs=P("gx", "gy", "gz", None),
        check_vma=False,
    )
```

```python
import functools

import jax
import jax.numpy as jnp
import ml_dtypes
import numpy as np
from jax import lax
from jax.experimental import pallas as pl
from jax.experimental.pallas import tpu as pltpu
from jax.sharding import PartitionSpec as P

POLY = 8
SIDE = POLY + 1
CENTER = 6.0
HALF_WIDTH = 8.0
MESH = pl.DeviceIdType.MESH
F32 = jnp.float32
BF16 = jnp.bfloat16
HIGHEST = lax.Precision.HIGHEST
TILE = 8

COLS = SIDE * SIDE * POLY
ROWS = 736
PLANE = ROWS - COLS
LINE = SIDE * POLY

DIRECTIONS = sorted(
    [
        (dx, dy, dz)
        for dx in (-1, 0, 1)
        for dy in (-1, 0, 1)
        for dz in (-1, 0, 1)
        if (dx, dy, dz) != (0, 0, 0)
    ],
    key=lambda d: -sum(map(abs, d)),
)
LOW = [d for d in DIRECTIONS if max(d) <= 0]
HIGH = [d for d in DIRECTIONS if min(d) >= 0]


def column_rows(d):
    if d[2] != 0:
        return 0
    return 2 * LINE if 0 in d[:2] else 2 * POLY


def plane_rows(d):
    return 96 if d[:2] == (0, 0) else 16


OFFSET = {}
_at = 0
for _d in DIRECTIONS:
    OFFSET[_d] = _at
    _at += column_rows(_d) + plane_rows(_d)
MESSAGE_ROWS = _at


def message_rows(dirs):
    return sum(column_rows(d) + plane_rows(d) for d in dirs)


TOP = [d for d in DIRECTIONS if d[2] <= 0]
BOTTOM = [d for d in DIRECTIONS if d[2] > 0]


def edge_nodes(step):
    return [8] if step > 0 else [0] if step < 0 else list(range(SIDE))


def plane_nodes(d):
    return [(i, j) for i in edge_nodes(d[0]) for j in edge_nodes(d[1])]


def tables():
    order = np.zeros((ROWS, SIDE**3), np.float32)
    for i in range(SIDE):
        for j in range(SIDE):
            for k in range(POLY):
                order[i * LINE + j * POLY + k, i * 81 + j * 9 + k] = 1
            order[COLS + i * 9 + j, i * 81 + j * 9 + POLY] = 1
    pick = np.zeros((sum(plane_rows(d) for d in DIRECTIONS), ROWS), np.float32)
    at = 0
    for d in DIRECTIONS:
        for t, (i, j) in enumerate(plane_nodes(d)):
            pick[at + t, i * LINE + j * POLY if d[2] < 0 else COLS + i * 9 + j] = 1
        at += plane_rows(d)
    top = np.zeros((PLANE, sum(plane_rows(d) for d in TOP)), np.float32)
    at = 0
    for d in TOP:
        for t, (i, j) in enumerate(plane_nodes((-d[0], -d[1], 0))):
            top[i * 9 + j, at + t] = 1
        at += plane_rows(d)
    bottom = np.zeros((COLS, sum(plane_rows(d) for d in BOTTOM)), np.float32)
    at = 0
    for d in BOTTOM:
        for t, (i, j) in enumerate(plane_nodes((-d[0], -d[1], 0))):
            bottom[i * LINE + j * POLY, at + t] = 1
        at += plane_rows(d)
    insert = np.zeros((COLS, PLANE), np.float32)
    for i in range(SIDE):
        for j in range(SIDE):
            insert[i * LINE + j * POLY, i * 9 + j] = 1
    made = [order, pick, top, bottom, np.concatenate([insert, insert], 1), insert.T]
    return [m.astype(ml_dtypes.bfloat16) for m in made]


def dot(a, b):
    return jnp.dot(a, b, preferred_element_type=F32)


def filter_kernel(
    sizes,
    *refs,
):
    operands = refs[:9]
    filtered_out, gram_out = refs[9:11]
    held = refs[11:20]
    (
        load_sem, store_sem, filtered, operator, shift, sums, field0, field1, field2, send, recv, total, parts, planes, whole,
        send_sem, recv_sem, part_send_sem, part_recv_sem,
    ) = refs[20:]
    orbitals, potential, pick, cell, order, top, insert, extract, bottom = held
    nx, ny, nz = sizes
    me = (lax.axis_index("gx"), lax.axis_index("gy"), lax.axis_index("gz"))
    group = nx * ny
    mine = me[0] * ny + me[1]
    chunk = total.shape[0] // group

    def towards(d):
        return tuple(
            m if s == 0 else lax.rem(m + (s + n), n) for m, s, n in zip(me, d, sizes)
        )

    def member(t):
        other = lax.rem(mine + t, group)
        return other, (other // ny, lax.rem(other, ny), me[2])

    def above(t):
        return me[0], me[1], lax.rem(me[2] + t, nz)

    def tile(n):
        return pl.ds(pl.multiple_of(n * chunk, chunk), chunk)

    barrier = pltpu.get_barrier_semaphore()
    for d in DIRECTIONS:
        pl.semaphore_signal(barrier, inc=1, device_id=towards(d), device_id_type=MESH)

    @pl.loop(1, group)
    def _(t):
        pl.semaphore_signal(barrier, inc=1, device_id=member(t)[1], device_id_type=MESH)

    @pl.loop(1, nz)
    def _(t):
        pl.semaphore_signal(barrier, inc=1, device_id=above(t), device_id_type=MESH)

    loads = [
        pltpu.make_async_copy(operand, place, load_sem.at[n])
        for n, (operand, place) in enumerate(zip(operands, held))
    ]
    for load in loads:
        load.start()

    def column_slices(d):
        for c in range(2):
            if d[1] == 0:
                yield c, (0 if d[0] < 0 else 8) * LINE, LINE
            else:
                for i in edge_nodes(d[0]):
                    yield c, i * LINE + (0 if d[1] < 0 else 8) * POLY, POLY

    def pack(number, dirs):
        source = jnp.concatenate([sums[0, :COLS], sums[1, COLS:]], axis=0).astype(BF16)
        small = dot(pick[...], source).astype(BF16)
        at = 0
        for d in DIRECTIONS:
            columns, width = column_rows(d), plane_rows(d)
            if d in dirs:
                if columns:
                    pieces = [sums[c, r : r + w] for c, r, w in column_slices(d)]
                    send[number, pl.ds(OFFSET[d], columns)] = jnp.concatenate(
                        pieces, axis=0
                    ).astype(BF16)
                send[number, pl.ds(OFFSET[d] + columns, width)] = small[at : at + width]
            at += width

    def copies(number, dirs):
        for d in dirs:
            rows = pl.ds(OFFSET[d], column_rows(d) + plane_rows(d))
            yield pltpu.make_async_remote_copy(
                src_ref=send.at[number, rows],
                dst_ref=recv.at[number, rows],
                send_sem=send_sem.at[number],
                recv_sem=recv_sem.at[number],
                device_id=towards(d),
                device_id_type=MESH,
            )

    def finish(number, dirs, semaphore):
        arrived = recv.at[number, pl.ds(0, message_rows(dirs))]
        pltpu.make_async_copy(arrived, arrived, semaphore.at[number]).wait()

    def unpack(number, dirs):
        for d in dirs:
            if column_rows(d):
                got = recv[number, pl.ds(OFFSET[d], column_rows(d))].astype(F32)
                at = 0
                for c, r, w in column_slices((-d[0], -d[1], 0)):
                    sums[c, r : r + w] += got[at : at + w]
                    at += w

        def plane_parts(wanted):
            return jnp.concatenate(
                [
                    recv[number, pl.ds(OFFSET[d] + column_rows(d), plane_rows(d))]
                    if d in dirs
                    else jnp.zeros((plane_rows(d), recv.shape[-1]), BF16)
                    for d in wanted
                ],
                axis=0,
            )

        if dirs is not HIGH:
            sums[1, COLS:] += dot(top[...], plane_parts(TOP))
        if dirs is not LOW:
            sums[0, :COLS] += dot(bottom[...], plane_parts(BOTTOM))

    def exchange(number, dirs, meanwhile=None):
        pack(number, dirs)
        for copy in copies(number, dirs):
            copy.start()
        if meanwhile is not None:
            meanwhile()
        finish(number, dirs, recv_sem)
        unpack(number, dirs)

    def hold(field, first, second, last):
        closing = dot(extract[...], second.astype(BF16))
        field[0] = jnp.concatenate([first, closing], axis=0).astype(BF16)
        field[1] = jnp.concatenate([second, last], axis=0).astype(BF16)

    def apply_operator(field):
        for c in range(2):
            values = field[c]
            image = dot(operator[...], values)
            sums[c, :COLS] = image[:COLS] + shift[c] * values.astype(F32)[:COLS]
            sums[c, COLS:] = image[COLS:]
        plane = sums[0, COLS:]
        high = plane.astype(BF16).astype(F32)
        split = jnp.concatenate([high, plane - high], axis=0).astype(BF16)
        sums[1, :COLS] += dot(insert[...], split)

    sums[...] = jnp.zeros_like(sums)
    shift[...] = jnp.zeros_like(shift)
    loads[0].wait()
    loads[1].wait()
    for i in range(POLY):
        layer = orbitals[i].astype(F32).reshape(POLY, 2, POLY, -1)
        scale = jnp.broadcast_to(
            (potential[i] - CENTER)[:, :, None], (POLY, 2 * POLY, layer.shape[-1])
        ).reshape(layer.shape)
        for c in range(2):
            sums[c, i * LINE : i * LINE + 64] = layer[:, c].reshape(64, -1)
            shift[c, i * LINE : i * LINE + 64] = scale[:, c].reshape(64, -1)

    def make_operator():
        for load in loads[3:]:
            load.wait()
        turned = dot(order[...], cell[...]).astype(BF16)
        operator[...] = lax.dot_general(
            turned, order[...], (((1,), (1,)), ((), ())), preferred_element_type=F32
        ).astype(BF16)

    loads[2].wait()
    pl.semaphore_wait(barrier, len(DIRECTIONS) + group - 1 + nz - 1)
    exchange(0, LOW, make_operator)
    hold(field0, sums[0, :COLS], sums[1, :COLS], sums[1, COLS:])

    apply_operator(field0)
    exchange(1, DIRECTIONS)
    scaled = [sums[c] / HALF_WIDTH for c in range(2)]
    hold(field1, scaled[0][:COLS], scaled[1][:COLS], scaled[1][COLS:])

    apply_operator(field1)
    exchange(2, DIRECTIONS)
    scaled = [2.0 * sums[c] / HALF_WIDTH - field0[c].astype(F32) for c in range(2)]
    hold(field2, scaled[0][:COLS], scaled[1][:COLS], scaled[1][COLS:])

    apply_operator(field2)
    exchange(3, HIGH)
    for i in range(POLY):
        rows = slice(i * LINE, i * LINE + 64)
        halves = []
        for c in range(2):
            before = field1[c].astype(F32)[rows]
            now = 2.0 * sums[c, rows] / HALF_WIDTH - before
            halves.append(now.reshape(POLY, 1, POLY, -1))
        layer = jnp.concatenate(halves, axis=1).reshape(POLY, 2 * POLY, -1)
        filtered[i] = layer.astype(BF16)

    store = pltpu.make_async_copy(filtered, filtered_out, store_sem.at[0])
    store.start()
    flat = filtered[...].reshape(-1, filtered.shape[-1])
    total[...] = lax.dot_general(
        flat, flat, (((0,), (0,)), ((), ())), preferred_element_type=F32
    )

    def part_copy(phase, source, target, device):
        return pltpu.make_async_remote_copy(
            src_ref=source,
            dst_ref=target,
            send_sem=part_send_sem.at[phase],
            recv_sem=part_recv_sem.at[phase],
            device_id=device,
            device_id_type=MESH,
        )

    def part_wait(buffer, count, semaphore):
        some = buffer.at[pl.ds(0, count)]
        pltpu.make_async_copy(some, some, semaphore).wait()

    @pl.loop(1, group)
    def _(t):
        other, device = member(t)
        part_copy(0, total.at[tile(other)], parts.at[mine], device).start()

    parts[mine] = total[tile(mine)]
    part_wait(parts, group - 1, part_recv_sem.at[0])
    planes[me[2]] = jnp.sum(parts[...], axis=0)

    @pl.loop(1, nz)
    def _(t):
        part_copy(1, planes.at[me[2]], planes.at[me[2]], above(t)).start()

    part_wait(planes, nz - 1, part_recv_sem.at[1])
    whole[tile(mine)] = jnp.sum(planes[...], axis=0)

    @pl.loop(1, group)
    def _(t):
        part_copy(2, whole.at[tile(mine)], whole.at[tile(mine)], member(t)[1]).start()

    part_wait(whole, (group - 1) * chunk, part_recv_sem.at[2])
    gram_store = pltpu.make_async_copy(whole, gram_out, store_sem.at[1])
    gram_store.start()

    for number, dirs in enumerate((LOW, DIRECTIONS, DIRECTIONS, HIGH)):
        finish(number, dirs, send_sem)
    part_wait(parts, group - 1, part_send_sem.at[0])
    part_wait(planes, nz - 1, part_send_sem.at[1])
    part_wait(whole, (group - 1) * chunk, part_send_sem.at[2])
    store.wait()
    gram_store.wait()


def filter_and_gram(sizes, orbitals, cell_block, potential):
    width = orbitals.shape[-1]
    group = sizes[0] * sizes[1]
    order, pick, top, bottom, insert, extract = tables()
    operands = [orbitals, potential, pick, cell_block, order, top, insert, extract, bottom]
    hbm = pl.BlockSpec(memory_space=pltpu.MemorySpace.HBM)
    return pl.pallas_call(
        functools.partial(filter_kernel, sizes),
        out_shape=[
            jax.ShapeDtypeStruct(orbitals.shape, BF16),
            jax.ShapeDtypeStruct((width, width), F32),
        ],
        in_specs=[hbm] * len(operands),
        out_specs=[hbm] * 2,
        scratch_shapes=[pltpu.VMEM(a.shape, a.dtype) for a in operands]
        + [
            pltpu.SemaphoreType.DMA((len(operands),)),
            pltpu.SemaphoreType.DMA((2,)),
            pltpu.VMEM(orbitals.shape, BF16),
            pltpu.VMEM((ROWS, ROWS), BF16),
            pltpu.VMEM((2, COLS, width), F32),
            pltpu.VMEM((2, ROWS, width), F32),
            pltpu.VMEM((2, ROWS, width), BF16),
            pltpu.VMEM((2, ROWS, width), BF16),
            pltpu.VMEM((2, ROWS, width), BF16),
            pltpu.VMEM((4, MESSAGE_ROWS, width), BF16),
            pltpu.VMEM((4, MESSAGE_ROWS, width), BF16),
            pltpu.VMEM((width, width), F32),
            pltpu.VMEM((group, width // group, width), F32),
            pltpu.VMEM((sizes[2], width // group, width), F32),
            pltpu.VMEM((width, width), F32),
            pltpu.SemaphoreType.DMA((4,)),
            pltpu.SemaphoreType.DMA((4,)),
            pltpu.SemaphoreType.DMA((3,)),
            pltpu.SemaphoreType.DMA((3,)),
        ],
        compiler_params=pltpu.CompilerParams(
            collective_id=0, has_side_effects=True, vmem_limit_bytes=62 * 2**20
        ),
    )(*operands)


def spread_lane(x, n):
    return jnp.broadcast_to(x[:, n : n + 1], x.shape)


def spread_row(x, n):
    return jnp.broadcast_to(x[n : n + 1], x.shape)


def inverse_factor(rows):
    count = len(rows)
    shape = rows[0].shape
    height = lax.broadcasted_iota(jnp.int32, shape, 0)
    lane = lax.broadcasted_iota(jnp.int32, shape, 1)
    rows = list(rows)
    made = [jnp.where(lane == height + TILE * g, 1.0, 0.0).astype(F32) for g in range(count)]
    for b in range(count):
        lead, image = rows[b], made[b]
        columns = [spread_lane(lead, TILE * b + t) for t in range(TILE)]
        recips, coefs, lead_rows, image_rows = [], [], [], []
        pivots = jnp.ones(shape, F32)
        for t in range(TILE):
            pivot = spread_row(columns[t], t)
            recips.append(1.0 / pivot)
            pivots = jnp.where(height == t, pivot, pivots)
            factor = jnp.where(height > t, columns[t] * recips[t], 0.0)
            coefs.append({u: spread_row(columns[u], t) for u in range(t + 1, TILE)})
            for u in range(t + 1, TILE):
                columns[u] = columns[u] - factor * coefs[t][u]
            lead_rows.append(spread_row(lead, t))
            image_rows.append(spread_row(image, t))
            lead = lead - factor * lead_rows[t]
            image = image - factor * image_rows[t]
        made[b] = image * lax.rsqrt(pivots)
        for g in range(b + 1, count):
            entries = [spread_lane(rows[g], TILE * b + t) for t in range(TILE)]
            for t in range(TILE):
                factor = entries[t] * recips[t]
                for u in range(t + 1, TILE):
                    entries[u] = entries[u] - factor * coefs[t][u]
                rows[g] = rows[g] - factor * lead_rows[t]
                made[g] = made[g] - factor * image_rows[t]
    return jnp.concatenate(made, axis=0)


def full(a, b, contract=((1,), (0,))):
    return lax.dot_general(a, b, (contract, ((), ())), precision=HIGHEST, preferred_element_type=F32)


NT = ((1,), (1,))


def rotate_kernel(node_total, gram_in, filtered_in, out, gram, filtered, load_sem):
    gram_load = pltpu.make_async_copy(gram_in, gram, load_sem.at[0])
    gram_load.start()
    load = pltpu.make_async_copy(filtered_in, filtered, load_sem.at[1])
    load.start()
    gram_load.wait()
    half = gram.shape[0] // 2
    scaled = gram[...] / node_total

    def groups(block):
        return [block[TILE * g : TILE * (g + 1)] for g in range(half // TILE)]

    first = inverse_factor(groups(scaled[:half, :half]))
    below = full(scaled[half:, :half], first, NT)
    second = inverse_factor(groups(scaled[half:, half:] - full(below, below, NT)))
    corner = -full(second, full(below, first))
    inverse = jnp.concatenate(
        [
            jnp.concatenate([first, jnp.zeros((half, half), F32)], axis=1),
            jnp.concatenate([corner, second], axis=1),
        ],
        axis=0,
    )
    high = inverse.astype(BF16)
    low = (inverse - high.astype(F32)).astype(BF16)
    load.wait()
    flat = filtered[...].reshape(-1, filtered.shape[-1])
    dims = (NT, ((), ()))
    rotated = lax.dot_general(flat, high, dims, preferred_element_type=F32) + lax.dot_general(
        flat, low, dims, preferred_element_type=F32
    )
    out[...] = rotated.astype(BF16).reshape(out.shape)


def rotate(node_total, gram, filtered):
    hbm = pl.BlockSpec(memory_space=pltpu.MemorySpace.HBM)
    return pl.pallas_call(
        functools.partial(rotate_kernel, node_total),
        out_shape=jax.ShapeDtypeStruct(filtered.shape, BF16),
        in_specs=[hbm] * 2,
        out_specs=pl.BlockSpec(memory_space=pltpu.VMEM),
        scratch_shapes=[
            pltpu.VMEM(gram.shape, F32),
            pltpu.VMEM(filtered.shape, BF16),
            pltpu.SemaphoreType.DMA((2,)),
        ],
        compiler_params=pltpu.CompilerParams(vmem_limit_bytes=62 * 2**20),
    )(gram, filtered)


def local(sizes, orbitals, cell_block, potential):
    filtered, gram = filter_and_gram(sizes, orbitals, cell_block, potential)
    node_total = filtered.size // filtered.shape[-1] * sizes[0] * sizes[1] * sizes[2]
    return rotate(node_total, gram, filtered)


def solution(mesh):
    sizes = tuple(mesh.shape[name] for name in ("gx", "gy", "gz"))
    placed = (P("gx", "gy", "gz", None), P(), P("gx", "gy", "gz"))
    return jax.shard_map(
        functools.partial(local, sizes),
        mesh=mesh,
        in_specs=placed,
        out_specs=P("gx", "gy", "gz", None),
        check_vma=False,
    )
```

```python
import functools

import jax
import jax.numpy as jnp
import ml_dtypes
import numpy as np
from jax import lax
from jax.experimental import pallas as pl
from jax.experimental.pallas import tpu as pltpu
from jax.sharding import PartitionSpec as P

POLY = 8
SIDE = POLY + 1
CENTER = 6.0
HALF_WIDTH = 8.0
MESH = pl.DeviceIdType.MESH
F32 = jnp.float32
BF16 = jnp.bfloat16
HIGHEST = lax.Precision.HIGHEST
TILE = 8

COLS = SIDE * SIDE * POLY
ROWS = 736
PLANE = ROWS - COLS
LINE = SIDE * POLY

DIRECTIONS = sorted(
    [
        (dx, dy, dz)
        for dx in (-1, 0, 1)
        for dy in (-1, 0, 1)
        for dz in (-1, 0, 1)
        if (dx, dy, dz) != (0, 0, 0)
    ],
    key=lambda d: -sum(map(abs, d)),
)
LOW = [d for d in DIRECTIONS if max(d) <= 0]
HIGH = [d for d in DIRECTIONS if min(d) >= 0]


def column_rows(d):
    if d[2] != 0:
        return 0
    return 2 * LINE if 0 in d[:2] else 2 * POLY


def plane_rows(d):
    return 96 if d[:2] == (0, 0) else 16


OFFSET = {}
_at = 0
for _d in DIRECTIONS:
    OFFSET[_d] = _at
    _at += column_rows(_d) + plane_rows(_d)
MESSAGE_ROWS = _at


def message_rows(dirs):
    return sum(column_rows(d) + plane_rows(d) for d in dirs)


TOP = [d for d in DIRECTIONS if d[2] <= 0]
BOTTOM = [d for d in DIRECTIONS if d[2] > 0]


def edge_nodes(step):
    return [8] if step > 0 else [0] if step < 0 else list(range(SIDE))


def plane_nodes(d):
    return [(i, j) for i in edge_nodes(d[0]) for j in edge_nodes(d[1])]


def tables():
    order = np.zeros((ROWS, SIDE**3), np.float32)
    for i in range(SIDE):
        for j in range(SIDE):
            for k in range(POLY):
                order[i * LINE + j * POLY + k, i * 81 + j * 9 + k] = 1
            order[COLS + i * 9 + j, i * 81 + j * 9 + POLY] = 1
    pick = np.zeros((sum(plane_rows(d) for d in DIRECTIONS), ROWS), np.float32)
    at = 0
    for d in DIRECTIONS:
        for t, (i, j) in enumerate(plane_nodes(d)):
            pick[at + t, i * LINE + j * POLY if d[2] < 0 else COLS + i * 9 + j] = 1
        at += plane_rows(d)
    top = np.zeros((PLANE, sum(plane_rows(d) for d in TOP)), np.float32)
    at = 0
    for d in TOP:
        for t, (i, j) in enumerate(plane_nodes((-d[0], -d[1], 0))):
            top[i * 9 + j, at + t] = 1
        at += plane_rows(d)
    bottom = np.zeros((COLS, sum(plane_rows(d) for d in BOTTOM)), np.float32)
    at = 0
    for d in BOTTOM:
        for t, (i, j) in enumerate(plane_nodes((-d[0], -d[1], 0))):
            bottom[i * LINE + j * POLY, at + t] = 1
        at += plane_rows(d)
    insert = np.zeros((COLS, PLANE), np.float32)
    for i in range(SIDE):
        for j in range(SIDE):
            insert[i * LINE + j * POLY, i * 9 + j] = 1
    made = [order, pick, top, bottom, np.concatenate([insert, insert], 1), insert.T]
    return [m.astype(ml_dtypes.bfloat16) for m in made]


def dot(a, b):
    return jnp.dot(a, b, preferred_element_type=F32)


def filter_kernel(
    sizes,
    *refs,
):
    operands = refs[:9]
    filtered_out, gram_out = refs[9:11]
    held = refs[11:20]
    (
        load_sem, store_sem, filtered, operator, shift, sums, field0, field1, field2, send, recv, total, parts, planes, whole,
        send_sem, recv_sem, part_send_sem, part_recv_sem,
    ) = refs[20:]
    orbitals, potential, pick, cell, order, top, insert, extract, bottom = held
    nx, ny, nz = sizes
    me = (lax.axis_index("gx"), lax.axis_index("gy"), lax.axis_index("gz"))
    group = nx * ny
    mine = me[0] * ny + me[1]
    chunk = total.shape[0] // group

    def towards(d):
        return tuple(
            m if s == 0 else lax.rem(m + (s + n), n) for m, s, n in zip(me, d, sizes)
        )

    def member(t):
        x, y = lax.rem(me[0] + t // ny, nx), lax.rem(me[1] + t % ny, ny)
        return x * ny + y, (x, y, me[2])

    def distance(t):
        x, y = t // ny, t % ny
        return min(x, nx - x) + min(y, ny - y) / 2

    farthest_first = sorted(range(1, group), key=distance, reverse=True)
    layers_farthest_first = sorted(range(1, nz), key=lambda t: -min(t, nz - t))

    def above(t):
        return me[0], me[1], lax.rem(me[2] + t, nz)

    def tile(n):
        return pl.ds(pl.multiple_of(n * chunk, chunk), chunk)

    barrier = pltpu.get_barrier_semaphore()
    for d in DIRECTIONS:
        pl.semaphore_signal(barrier, inc=1, device_id=towards(d), device_id_type=MESH)

    loads = [
        pltpu.make_async_copy(operand, place, load_sem.at[n])
        for n, (operand, place) in enumerate(zip(operands, held))
    ]
    for load in loads:
        load.start()

    def column_slices(d):
        for c in range(2):
            if d[1] == 0:
                yield c, (0 if d[0] < 0 else 8) * LINE, LINE
            else:
                for i in edge_nodes(d[0]):
                    yield c, i * LINE + (0 if d[1] < 0 else 8) * POLY, POLY

    def pack(number, dirs):
        source = jnp.concatenate([sums[0, :COLS], sums[1, COLS:]], axis=0).astype(BF16)
        small = dot(pick[...], source).astype(BF16)
        at = 0
        for d in DIRECTIONS:
            columns, width = column_rows(d), plane_rows(d)
            if d in dirs:
                if columns:
                    pieces = [sums[c, r : r + w] for c, r, w in column_slices(d)]
                    send[number, pl.ds(OFFSET[d], columns)] = jnp.concatenate(
                        pieces, axis=0
                    ).astype(BF16)
                send[number, pl.ds(OFFSET[d] + columns, width)] = small[at : at + width]
            at += width

    def copies(number, dirs):
        for d in dirs:
            rows = pl.ds(OFFSET[d], column_rows(d) + plane_rows(d))
            yield pltpu.make_async_remote_copy(
                src_ref=send.at[number, rows],
                dst_ref=recv.at[number, rows],
                send_sem=send_sem.at[number],
                recv_sem=recv_sem.at[number],
                device_id=towards(d),
                device_id_type=MESH,
            )

    def finish(number, dirs, semaphore):
        arrived = recv.at[number, pl.ds(0, message_rows(dirs))]
        pltpu.make_async_copy(arrived, arrived, semaphore.at[number]).wait()

    def unpack(number, dirs):
        for d in dirs:
            if column_rows(d):
                got = recv[number, pl.ds(OFFSET[d], column_rows(d))].astype(F32)
                at = 0
                for c, r, w in column_slices((-d[0], -d[1], 0)):
                    sums[c, r : r + w] += got[at : at + w]
                    at += w

        def plane_parts(wanted):
            return jnp.concatenate(
                [
                    recv[number, pl.ds(OFFSET[d] + column_rows(d), plane_rows(d))]
                    if d in dirs
                    else jnp.zeros((plane_rows(d), recv.shape[-1]), BF16)
                    for d in wanted
                ],
                axis=0,
            )

        if dirs is not HIGH:
            sums[1, COLS:] += dot(top[...], plane_parts(TOP))
        if dirs is not LOW:
            sums[0, :COLS] += dot(bottom[...], plane_parts(BOTTOM))

    def exchange(number, dirs, meanwhile=None):
        pack(number, dirs)
        for copy in copies(number, dirs):
            copy.start()
        if meanwhile is not None:
            meanwhile()
        finish(number, dirs, recv_sem)
        unpack(number, dirs)

    def hold(field, first, second, last):
        closing = dot(extract[...], second.astype(BF16))
        field[0] = jnp.concatenate([first, closing], axis=0).astype(BF16)
        field[1] = jnp.concatenate([second, last], axis=0).astype(BF16)

    def apply_operator(field):
        for c in range(2):
            values = field[c]
            image = dot(operator[...], values)
            sums[c, :COLS] = image[:COLS] + shift[c] * values.astype(F32)[:COLS]
            sums[c, COLS:] = image[COLS:]
        plane = sums[0, COLS:]
        high = plane.astype(BF16).astype(F32)
        split = jnp.concatenate([high, plane - high], axis=0).astype(BF16)
        sums[1, :COLS] += dot(insert[...], split)

    sums[...] = jnp.zeros_like(sums)
    loads[0].wait()
    for i in range(POLY):
        layer = orbitals[i].astype(F32).reshape(POLY, 2, POLY, -1)
        for c in range(2):
            sums[c, i * LINE : i * LINE + 64] = layer[:, c].reshape(64, -1)

    def make_operator():
        loads[1].wait()
        shift[...] = jnp.zeros_like(shift)
        for i in range(POLY):
            scale = jnp.broadcast_to(
                (potential[i] - CENTER)[:, :, None], (POLY, 2 * POLY, shift.shape[-1])
            ).reshape(POLY, 2, POLY, -1)
            for c in range(2):
                shift[c, i * LINE : i * LINE + 64] = scale[:, c].reshape(64, -1)
        for load in loads[3:]:
            load.wait()
        turned = dot(order[...], cell[...]).astype(BF16)
        operator[...] = lax.dot_general(
            turned, order[...], (((1,), (1,)), ((), ())), preferred_element_type=F32
        ).astype(BF16)

    loads[2].wait()
    pl.semaphore_wait(barrier, len(DIRECTIONS))
    exchange(0, LOW, make_operator)
    hold(field0, sums[0, :COLS], sums[1, :COLS], sums[1, COLS:])

    apply_operator(field0)
    exchange(1, DIRECTIONS)
    scaled = [sums[c] / HALF_WIDTH for c in range(2)]
    hold(field1, scaled[0][:COLS], scaled[1][:COLS], scaled[1][COLS:])

    apply_operator(field1)
    exchange(2, DIRECTIONS)
    scaled = [2.0 * sums[c] / HALF_WIDTH - field0[c].astype(F32) for c in range(2)]
    hold(field2, scaled[0][:COLS], scaled[1][:COLS], scaled[1][COLS:])

    apply_operator(field2)
    exchange(3, HIGH)
    for i in range(POLY):
        rows = slice(i * LINE, i * LINE + 64)
        halves = []
        for c in range(2):
            before = field1[c].astype(F32)[rows]
            now = 2.0 * sums[c, rows] / HALF_WIDTH - before
            halves.append(now.reshape(POLY, 1, POLY, -1))
        layer = jnp.concatenate(halves, axis=1).reshape(POLY, 2 * POLY, -1)
        filtered[i] = layer.astype(BF16)

    store = pltpu.make_async_copy(filtered, filtered_out, store_sem.at[0])
    store.start()
    flat = filtered[...].reshape(-1, filtered.shape[-1])
    total[...] = lax.dot_general(
        flat, flat, (((0,), (0,)), ((), ())), preferred_element_type=F32
    )

    def part_copy(phase, source, target, device):
        return pltpu.make_async_remote_copy(
            src_ref=source,
            dst_ref=target,
            send_sem=part_send_sem.at[phase],
            recv_sem=part_recv_sem.at[phase],
            device_id=device,
            device_id_type=MESH,
        )

    def part_wait(buffer, count, semaphore):
        some = buffer.at[pl.ds(0, count)]
        pltpu.make_async_copy(some, some, semaphore).wait()

    for t in farthest_first:
        other, device = member(t)
        part_copy(0, total.at[tile(other)], parts.at[mine], device).start()

    parts[mine] = total[tile(mine)]
    part_wait(parts, group - 1, part_recv_sem.at[0])
    planes[me[2]] = jnp.sum(parts[...], axis=0)

    for t in layers_farthest_first:
        part_copy(1, planes.at[me[2]], planes.at[me[2]], above(t)).start()

    part_wait(planes, nz - 1, part_recv_sem.at[1])
    whole[tile(mine)] = jnp.sum(planes[...], axis=0)

    for t in farthest_first:
        part_copy(2, whole.at[tile(mine)], whole.at[tile(mine)], member(t)[1]).start()

    part_wait(whole, (group - 1) * chunk, part_recv_sem.at[2])
    gram_store = pltpu.make_async_copy(whole, gram_out, store_sem.at[1])
    gram_store.start()

    for number, dirs in enumerate((LOW, DIRECTIONS, DIRECTIONS, HIGH)):
        finish(number, dirs, send_sem)
    part_wait(parts, group - 1, part_send_sem.at[0])
    part_wait(planes, nz - 1, part_send_sem.at[1])
    part_wait(whole, (group - 1) * chunk, part_send_sem.at[2])
    store.wait()
    gram_store.wait()


def filter_and_gram(sizes, orbitals, cell_block, potential):
    width = orbitals.shape[-1]
    group = sizes[0] * sizes[1]
    order, pick, top, bottom, insert, extract = tables()
    operands = [orbitals, potential, pick, cell_block, order, top, insert, extract, bottom]
    hbm = pl.BlockSpec(memory_space=pltpu.MemorySpace.HBM)
    return pl.pallas_call(
        functools.partial(filter_kernel, sizes),
        out_shape=[
            jax.ShapeDtypeStruct(orbitals.shape, BF16),
            jax.ShapeDtypeStruct((width, width), F32),
        ],
        in_specs=[hbm] * len(operands),
        out_specs=[hbm] * 2,
        scratch_shapes=[pltpu.VMEM(a.shape, a.dtype) for a in operands]
        + [
            pltpu.SemaphoreType.DMA((len(operands),)),
            pltpu.SemaphoreType.DMA((2,)),
            pltpu.VMEM(orbitals.shape, BF16),
            pltpu.VMEM((ROWS, ROWS), BF16),
            pltpu.VMEM((2, COLS, width), F32),
            pltpu.VMEM((2, ROWS, width), F32),
            pltpu.VMEM((2, ROWS, width), BF16),
            pltpu.VMEM((2, ROWS, width), BF16),
            pltpu.VMEM((2, ROWS, width), BF16),
            pltpu.VMEM((4, MESSAGE_ROWS, width), BF16),
            pltpu.VMEM((4, MESSAGE_ROWS, width), BF16),
            pltpu.VMEM((width, width), F32),
            pltpu.VMEM((group, width // group, width), F32),
            pltpu.VMEM((sizes[2], width // group, width), F32),
            pltpu.VMEM((width, width), F32),
            pltpu.SemaphoreType.DMA((4,)),
            pltpu.SemaphoreType.DMA((4,)),
            pltpu.SemaphoreType.DMA((3,)),
            pltpu.SemaphoreType.DMA((3,)),
        ],
        compiler_params=pltpu.CompilerParams(
            collective_id=0, has_side_effects=True, vmem_limit_bytes=62 * 2**20
        ),
    )(*operands)


def spread_lane(x, n):
    return jnp.broadcast_to(x[:, n : n + 1], x.shape)


def spread_row(x, n):
    return jnp.broadcast_to(x[n : n + 1], x.shape)


def inverse_factor(rows):
    count = len(rows)
    shape = rows[0].shape
    height = lax.broadcasted_iota(jnp.int32, shape, 0)
    lane = lax.broadcasted_iota(jnp.int32, shape, 1)
    rows = list(rows)
    made = [jnp.where(lane == height + TILE * g, 1.0, 0.0).astype(F32) for g in range(count)]
    for b in range(count):
        lead, image = rows[b], made[b]
        columns = [spread_lane(lead, TILE * b + t) for t in range(TILE)]
        recips, coefs, lead_rows, image_rows = [], [], [], []
        pivots = jnp.ones(shape, F32)
        for t in range(TILE):
            pivot = spread_row(columns[t], t)
            recips.append(1.0 / pivot)
            pivots = jnp.where(height == t, pivot, pivots)
            factor = jnp.where(height > t, columns[t] * recips[t], 0.0)
            coefs.append({u: spread_row(columns[u], t) for u in range(t + 1, TILE)})
            for u in range(t + 1, TILE):
                columns[u] = columns[u] - factor * coefs[t][u]
            lead_rows.append(spread_row(lead, t))
            image_rows.append(spread_row(image, t))
            lead = lead - factor * lead_rows[t]
            image = image - factor * image_rows[t]
        made[b] = image * lax.rsqrt(pivots)
        for g in range(b + 1, count):
            entries = [spread_lane(rows[g], TILE * b + t) for t in range(TILE)]
            for t in range(TILE):
                factor = entries[t] * recips[t]
                for u in range(t + 1, TILE):
                    entries[u] = entries[u] - factor * coefs[t][u]
                rows[g] = rows[g] - factor * lead_rows[t]
                made[g] = made[g] - factor * image_rows[t]
    return jnp.concatenate(made, axis=0)


def full(a, b, contract=((1,), (0,))):
    return lax.dot_general(a, b, (contract, ((), ())), precision=HIGHEST, preferred_element_type=F32)


NT = ((1,), (1,))


def rotate_kernel(node_total, gram_in, filtered_in, out, gram, filtered, made, load_sem, store_sem):
    gram_load = pltpu.make_async_copy(gram_in, gram, load_sem.at[0])
    gram_load.start()
    load = pltpu.make_async_copy(filtered_in, filtered, load_sem.at[1])
    load.start()
    gram_load.wait()
    half = gram.shape[0] // 2
    scaled = gram[...] / node_total

    def groups(block):
        return [block[TILE * g : TILE * (g + 1)] for g in range(half // TILE)]

    def rotated(values, factor):
        high = factor.astype(BF16).astype(F32)
        both = jnp.concatenate([high, factor - high], axis=0).astype(BF16)
        image = lax.dot_general(values, both, (NT, ((), ())), preferred_element_type=F32)
        return (image[:, :half] + image[:, half:]).astype(BF16)

    first = inverse_factor(groups(scaled[:half, :half]))
    below = full(scaled[half:, :half], first, NT)
    rest = scaled[half:, half:] - full(below, below, NT)
    load.wait()
    left = filtered[..., :half].reshape(-1, half)
    made[..., :half] = rotated(left, first).reshape(made.shape[:-1] + (half,))
    stores = [
        pltpu.make_async_copy(made.at[..., pl.ds(0, half)], out.at[..., pl.ds(0, half)], store_sem.at[0])
    ]
    stores[0].start()
    second = inverse_factor(groups(rest))
    corner = -full(second, full(below, first))
    bottom = jnp.concatenate([corner, second], axis=1)
    parts = 4
    step = made.shape[0] // parts
    for n in range(parts):
        block = filtered[n * step : (n + 1) * step]
        image = rotated(block.reshape(-1, block.shape[-1]), bottom)
        made[n * step : (n + 1) * step, :, :, half:] = image.reshape(block.shape[:-1] + (half,))
        where = (pl.ds(n * step, step), slice(None), slice(None), pl.ds(half, half))
        stores.append(pltpu.make_async_copy(made.at[where], out.at[where], store_sem.at[n + 1]))
        stores[-1].start()
    for store in stores:
        store.wait()


def rotate(node_total, gram, filtered):
    hbm = pl.BlockSpec(memory_space=pltpu.MemorySpace.HBM)
    return pl.pallas_call(
        functools.partial(rotate_kernel, node_total),
        out_shape=jax.ShapeDtypeStruct(filtered.shape, BF16),
        in_specs=[hbm] * 2,
        out_specs=hbm,
        scratch_shapes=[
            pltpu.VMEM(gram.shape, F32),
            pltpu.VMEM(filtered.shape, BF16),
            pltpu.VMEM(filtered.shape, BF16),
            pltpu.SemaphoreType.DMA((2,)),
            pltpu.SemaphoreType.DMA((5,)),
        ],
        compiler_params=pltpu.CompilerParams(vmem_limit_bytes=62 * 2**20),
    )(gram, filtered)


def local(sizes, orbitals, cell_block, potential):
    filtered, gram = filter_and_gram(sizes, orbitals, cell_block, potential)
    node_total = filtered.size // filtered.shape[-1] * sizes[0] * sizes[1] * sizes[2]
    return rotate(node_total, gram, filtered)


def solution(mesh):
    sizes = tuple(mesh.shape[name] for name in ("gx", "gy", "gz"))
    placed = (P("gx", "gy", "gz", None), P(), P("gx", "gy", "gz"))
    return jax.shard_map(
        functools.partial(local, sizes),
        mesh=mesh,
        in_specs=placed,
        out_specs=P("gx", "gy", "gz", None),
        check_vma=False,
    )
```

```python
import functools

import jax
import jax.numpy as jnp
import ml_dtypes
import numpy as np
from jax import lax
from jax.experimental import pallas as pl
from jax.experimental.pallas import tpu as pltpu
from jax.sharding import PartitionSpec as P

POLY = 8
SIDE = POLY + 1
CENTER = 6.0
HALF_WIDTH = 8.0
MESH = pl.DeviceIdType.MESH
F32 = jnp.float32
BF16 = jnp.bfloat16
HIGHEST = lax.Precision.HIGHEST
TILE = 8

COLS = SIDE * SIDE * POLY
ROWS = 736
PLANE = ROWS - COLS
LINE = SIDE * POLY

DIRECTIONS = sorted(
    [
        (dx, dy, dz)
        for dx in (-1, 0, 1)
        for dy in (-1, 0, 1)
        for dz in (-1, 0, 1)
        if (dx, dy, dz) != (0, 0, 0)
    ],
    key=lambda d: -sum(map(abs, d)),
)
LOW = [d for d in DIRECTIONS if max(d) <= 0]
HIGH = [d for d in DIRECTIONS if min(d) >= 0]


def column_rows(d):
    if d[2] != 0:
        return 0
    return 2 * LINE if 0 in d[:2] else 2 * POLY


def plane_rows(d):
    return 96 if d[:2] == (0, 0) else 16


OFFSET = {}
_at = 0
for _d in DIRECTIONS:
    OFFSET[_d] = _at
    _at += column_rows(_d) + plane_rows(_d)
MESSAGE_ROWS = _at


def message_rows(dirs):
    return sum(column_rows(d) + plane_rows(d) for d in dirs)


TOP = [d for d in DIRECTIONS if d[2] <= 0]
BOTTOM = [d for d in DIRECTIONS if d[2] > 0]


def edge_nodes(step):
    return [8] if step > 0 else [0] if step < 0 else list(range(SIDE))


def plane_nodes(d):
    return [(i, j) for i in edge_nodes(d[0]) for j in edge_nodes(d[1])]


def tables():
    order = np.zeros((ROWS, SIDE**3), np.float32)
    for i in range(SIDE):
        for j in range(SIDE):
            for k in range(POLY):
                order[i * LINE + j * POLY + k, i * 81 + j * 9 + k] = 1
            order[COLS + i * 9 + j, i * 81 + j * 9 + POLY] = 1
    pick = np.zeros((sum(plane_rows(d) for d in DIRECTIONS), ROWS), np.float32)
    at = 0
    for d in DIRECTIONS:
        for t, (i, j) in enumerate(plane_nodes(d)):
            pick[at + t, i * LINE + j * POLY if d[2] < 0 else COLS + i * 9 + j] = 1
        at += plane_rows(d)
    top = np.zeros((PLANE, sum(plane_rows(d) for d in TOP)), np.float32)
    at = 0
    for d in TOP:
        for t, (i, j) in enumerate(plane_nodes((-d[0], -d[1], 0))):
            top[i * 9 + j, at + t] = 1
        at += plane_rows(d)
    bottom = np.zeros((COLS, sum(plane_rows(d) for d in BOTTOM)), np.float32)
    at = 0
    for d in BOTTOM:
        for t, (i, j) in enumerate(plane_nodes((-d[0], -d[1], 0))):
            bottom[i * LINE + j * POLY, at + t] = 1
        at += plane_rows(d)
    insert = np.zeros((COLS, PLANE), np.float32)
    for i in range(SIDE):
        for j in range(SIDE):
            insert[i * LINE + j * POLY, i * 9 + j] = 1
    made = [order, pick, top, bottom, np.concatenate([insert, insert], 1), insert.T]
    return [m.astype(ml_dtypes.bfloat16) for m in made]


def dot(a, b):
    return jnp.dot(a, b, preferred_element_type=F32)


def filter_kernel(
    sizes,
    *refs,
):
    operands = refs[:9]
    filtered_out, gram_out = refs[9:11]
    held = refs[11:20]
    (
        load_sem, store_sem, filtered, operator, shift, sums, field0, field1, field2, send, recv, total, parts, planes, whole,
        send_sem, recv_sem, part_send_sem, part_recv_sem,
    ) = refs[20:]
    orbitals, potential, pick, cell, order, top, insert, extract, bottom = held
    nx, ny, nz = sizes
    me = (lax.axis_index("gx"), lax.axis_index("gy"), lax.axis_index("gz"))
    group = nx * ny
    mine = me[0] * ny + me[1]
    chunk = total.shape[0] // group

    def towards(d):
        return tuple(
            m if s == 0 else lax.rem(m + (s + n), n) for m, s, n in zip(me, d, sizes)
        )

    def member(t):
        x, y = lax.rem(me[0] + t // ny, nx), lax.rem(me[1] + t % ny, ny)
        return x * ny + y, (x, y, me[2])

    def distance(t):
        x, y = t // ny, t % ny
        return min(x, nx - x) + min(y, ny - y) / 2

    farthest_first = sorted(range(1, group), key=distance, reverse=True)
    layers_farthest_first = sorted(range(1, nz), key=lambda t: -min(t, nz - t))

    def above(t):
        return me[0], me[1], lax.rem(me[2] + t, nz)

    def tile(n):
        return pl.ds(pl.multiple_of(n * chunk, chunk), chunk)

    barrier = pltpu.get_barrier_semaphore()
    for d in DIRECTIONS:
        pl.semaphore_signal(barrier, inc=1, device_id=towards(d), device_id_type=MESH)

    loads = [
        pltpu.make_async_copy(operand, place, load_sem.at[n])
        for n, (operand, place) in enumerate(zip(operands, held))
    ]
    for load in loads:
        load.start()

    def column_slices(d):
        for c in range(2):
            if d[1] == 0:
                yield c, (0 if d[0] < 0 else 8) * LINE, LINE
            else:
                for i in edge_nodes(d[0]):
                    yield c, i * LINE + (0 if d[1] < 0 else 8) * POLY, POLY

    def pack(number, dirs):
        source = jnp.concatenate([sums[0, :COLS], sums[1, COLS:]], axis=0).astype(BF16)
        small = dot(pick[...], source).astype(BF16)
        at = 0
        for d in DIRECTIONS:
            columns, width = column_rows(d), plane_rows(d)
            if d in dirs:
                if columns:
                    pieces = [sums[c, r : r + w] for c, r, w in column_slices(d)]
                    send[number, pl.ds(OFFSET[d], columns)] = jnp.concatenate(
                        pieces, axis=0
                    ).astype(BF16)
                send[number, pl.ds(OFFSET[d] + columns, width)] = small[at : at + width]
            at += width

    def copies(number, dirs):
        for d in dirs:
            rows = pl.ds(OFFSET[d], column_rows(d) + plane_rows(d))
            yield pltpu.make_async_remote_copy(
                src_ref=send.at[number, rows],
                dst_ref=recv.at[number, rows],
                send_sem=send_sem.at[number],
                recv_sem=recv_sem.at[number],
                device_id=towards(d),
                device_id_type=MESH,
            )

    def finish(number, dirs, semaphore):
        arrived = recv.at[number, pl.ds(0, message_rows(dirs))]
        pltpu.make_async_copy(arrived, arrived, semaphore.at[number]).wait()

    def unpack(number, dirs):
        for d in dirs:
            if column_rows(d):
                got = recv[number, pl.ds(OFFSET[d], column_rows(d))].astype(F32)
                at = 0
                for c, r, w in column_slices((-d[0], -d[1], 0)):
                    sums[c, r : r + w] += got[at : at + w]
                    at += w

        def plane_parts(wanted):
            return jnp.concatenate(
                [
                    recv[number, pl.ds(OFFSET[d] + column_rows(d), plane_rows(d))]
                    if d in dirs
                    else jnp.zeros((plane_rows(d), recv.shape[-1]), BF16)
                    for d in wanted
                ],
                axis=0,
            )

        if dirs is not HIGH:
            sums[1, COLS:] += dot(top[...], plane_parts(TOP))
        if dirs is not LOW:
            sums[0, :COLS] += dot(bottom[...], plane_parts(BOTTOM))

    def exchange(number, dirs, meanwhile=None):
        pack(number, dirs)
        for copy in copies(number, dirs):
            copy.start()
        if meanwhile is not None:
            meanwhile()
        finish(number, dirs, recv_sem)
        unpack(number, dirs)

    def hold(field, first, second, last):
        closing = dot(extract[...], second.astype(BF16))
        field[0] = jnp.concatenate([first, closing], axis=0).astype(BF16)
        field[1] = jnp.concatenate([second, last], axis=0).astype(BF16)

    def apply_operator(field):
        for c in range(2):
            values = field[c]
            image = dot(operator[...], values)
            sums[c, :COLS] = image[:COLS] + shift[c] * values.astype(F32)[:COLS]
            sums[c, COLS:] = image[COLS:]
        plane = sums[0, COLS:]
        high = plane.astype(BF16).astype(F32)
        split = jnp.concatenate([high, plane - high], axis=0).astype(BF16)
        sums[1, :COLS] += dot(insert[...], split)

    sums[...] = jnp.zeros_like(sums)
    loads[0].wait()
    for i in range(POLY):
        layer = orbitals[i].astype(F32).reshape(POLY, 2, POLY, -1)
        for c in range(2):
            sums[c, i * LINE : i * LINE + 64] = layer[:, c].reshape(64, -1)

    def make_operator():
        loads[1].wait()
        shift[...] = jnp.zeros_like(shift)
        for i in range(POLY):
            scale = jnp.broadcast_to(
                (potential[i] - CENTER)[:, :, None], (POLY, 2 * POLY, shift.shape[-1])
            ).reshape(POLY, 2, POLY, -1)
            for c in range(2):
                shift[c, i * LINE : i * LINE + 64] = scale[:, c].reshape(64, -1)
        for load in loads[3:]:
            load.wait()
        turned = dot(order[...], cell[...]).astype(BF16)
        operator[...] = lax.dot_general(
            turned, order[...], (((1,), (1,)), ((), ())), preferred_element_type=F32
        ).astype(BF16)

    loads[2].wait()
    pl.semaphore_wait(barrier, len(DIRECTIONS))
    exchange(0, LOW, make_operator)
    hold(field0, sums[0, :COLS], sums[1, :COLS], sums[1, COLS:])

    apply_operator(field0)
    exchange(1, DIRECTIONS)
    scaled = [sums[c] / HALF_WIDTH for c in range(2)]
    hold(field1, scaled[0][:COLS], scaled[1][:COLS], scaled[1][COLS:])

    apply_operator(field1)
    exchange(2, DIRECTIONS)
    scaled = [2.0 * sums[c] / HALF_WIDTH - field0[c].astype(F32) for c in range(2)]
    hold(field2, scaled[0][:COLS], scaled[1][:COLS], scaled[1][COLS:])

    apply_operator(field2)
    exchange(3, HIGH)
    for i in range(POLY):
        rows = slice(i * LINE, i * LINE + 64)
        halves = []
        for c in range(2):
            before = field1[c].astype(F32)[rows]
            now = 2.0 * sums[c, rows] / HALF_WIDTH - before
            halves.append(now.reshape(POLY, 1, POLY, -1))
        layer = jnp.concatenate(halves, axis=1).reshape(POLY, 2 * POLY, -1)
        filtered[i] = layer.astype(BF16)

    store = pltpu.make_async_copy(filtered, filtered_out, store_sem.at[0])
    store.start()
    flat = filtered[...].reshape(-1, filtered.shape[-1])
    total[...] = lax.dot_general(
        flat, flat, (((0,), (0,)), ((), ())), preferred_element_type=F32
    )

    def part_copy(phase, source, target, device):
        return pltpu.make_async_remote_copy(
            src_ref=source,
            dst_ref=target,
            send_sem=part_send_sem.at[phase],
            recv_sem=part_recv_sem.at[phase],
            device_id=device,
            device_id_type=MESH,
        )

    def part_wait(buffer, count, semaphore):
        some = buffer.at[pl.ds(0, count)]
        pltpu.make_async_copy(some, some, semaphore).wait()

    for t in farthest_first:
        other, device = member(t)
        part_copy(0, total.at[tile(other)], parts.at[mine], device).start()

    parts[mine] = total[tile(mine)]
    part_wait(parts, group - 1, part_recv_sem.at[0])
    planes[me[2]] = jnp.sum(parts[...], axis=0)

    for t in layers_farthest_first:
        part_copy(1, planes.at[me[2]], planes.at[me[2]], above(t)).start()

    part_wait(planes, nz - 1, part_recv_sem.at[1])
    whole[...] = jnp.sum(planes[...], axis=0)
    gram_store = pltpu.make_async_copy(whole, gram_out.at[tile(mine)], store_sem.at[1])

    for t in farthest_first:
        part_copy(2, whole, gram_out.at[tile(mine)], member(t)[1]).start()

    gram_store.start()
    part_wait(gram_out, (group - 1) * chunk, part_recv_sem.at[2])

    for number, dirs in enumerate((LOW, DIRECTIONS, DIRECTIONS, HIGH)):
        finish(number, dirs, send_sem)
    part_wait(parts, group - 1, part_send_sem.at[0])
    part_wait(planes, nz - 1, part_send_sem.at[1])
    part_wait(gram_out, (group - 1) * chunk, part_send_sem.at[2])
    store.wait()
    gram_store.wait()


def filter_and_gram(sizes, orbitals, cell_block, potential):
    width = orbitals.shape[-1]
    group = sizes[0] * sizes[1]
    order, pick, top, bottom, insert, extract = tables()
    operands = [orbitals, potential, pick, cell_block, order, top, insert, extract, bottom]
    hbm = pl.BlockSpec(memory_space=pltpu.MemorySpace.HBM)
    return pl.pallas_call(
        functools.partial(filter_kernel, sizes),
        out_shape=[
            jax.ShapeDtypeStruct(orbitals.shape, BF16),
            jax.ShapeDtypeStruct((width, width), F32),
        ],
        in_specs=[hbm] * len(operands),
        out_specs=[hbm] * 2,
        scratch_shapes=[pltpu.VMEM(a.shape, a.dtype) for a in operands]
        + [
            pltpu.SemaphoreType.DMA((len(operands),)),
            pltpu.SemaphoreType.DMA((2,)),
            pltpu.VMEM(orbitals.shape, BF16),
            pltpu.VMEM((ROWS, ROWS), BF16),
            pltpu.VMEM((2, COLS, width), F32),
            pltpu.VMEM((2, ROWS, width), F32),
            pltpu.VMEM((2, ROWS, width), BF16),
            pltpu.VMEM((2, ROWS, width), BF16),
            pltpu.VMEM((2, ROWS, width), BF16),
            pltpu.VMEM((4, MESSAGE_ROWS, width), BF16),
            pltpu.VMEM((4, MESSAGE_ROWS, width), BF16),
            pltpu.VMEM((width, width), F32),
            pltpu.VMEM((group, width // group, width), F32),
            pltpu.VMEM((sizes[2], width // group, width), F32),
            pltpu.VMEM((width // group, width), F32),
            pltpu.SemaphoreType.DMA((4,)),
            pltpu.SemaphoreType.DMA((4,)),
            pltpu.SemaphoreType.DMA((3,)),
            pltpu.SemaphoreType.DMA((3,)),
        ],
        compiler_params=pltpu.CompilerParams(
            collective_id=0, has_side_effects=True, vmem_limit_bytes=62 * 2**20
        ),
    )(*operands)


def spread_lane(x, n):
    return jnp.broadcast_to(x[:, n : n + 1], x.shape)


def spread_row(x, n):
    return jnp.broadcast_to(x[n : n + 1], x.shape)


def inverse_factor(rows):
    count = len(rows)
    shape = rows[0].shape
    height = lax.broadcasted_iota(jnp.int32, shape, 0)
    lane = lax.broadcasted_iota(jnp.int32, shape, 1)
    rows = list(rows)
    made = [jnp.where(lane == height + TILE * g, 1.0, 0.0).astype(F32) for g in range(count)]
    for b in range(count):
        lead, image = rows[b], made[b]
        columns = [spread_lane(lead, TILE * b + t) for t in range(TILE)]
        recips, coefs, lead_rows, image_rows = [], [], [], []
        pivots = jnp.ones(shape, F32)
        for t in range(TILE):
            pivot = spread_row(columns[t], t)
            recips.append(1.0 / pivot)
            pivots = jnp.where(height == t, pivot, pivots)
            factor = jnp.where(height > t, columns[t] * recips[t], 0.0)
            coefs.append({u: spread_row(columns[u], t) for u in range(t + 1, TILE)})
            for u in range(t + 1, TILE):
                columns[u] = columns[u] - factor * coefs[t][u]
            lead_rows.append(spread_row(lead, t))
            image_rows.append(spread_row(image, t))
            lead = lead - factor * lead_rows[t]
            image = image - factor * image_rows[t]
        made[b] = image * lax.rsqrt(pivots)
        for g in range(b + 1, count):
            entries = [spread_lane(rows[g], TILE * b + t) for t in range(TILE)]
            for t in range(TILE):
                factor = entries[t] * recips[t]
                for u in range(t + 1, TILE):
                    entries[u] = entries[u] - factor * coefs[t][u]
                rows[g] = rows[g] - factor * lead_rows[t]
                made[g] = made[g] - factor * image_rows[t]
    return jnp.concatenate(made, axis=0)


def full(a, b, contract=((1,), (0,))):
    return lax.dot_general(a, b, (contract, ((), ())), precision=HIGHEST, preferred_element_type=F32)


NT = ((1,), (1,))


def rotate_kernel(node_total, gram_in, filtered_in, out, gram, filtered, made, load_sem, store_sem):
    gram_load = pltpu.make_async_copy(gram_in, gram, load_sem.at[0])
    gram_load.start()
    load = pltpu.make_async_copy(filtered_in, filtered, load_sem.at[1])
    load.start()
    gram_load.wait()
    half = gram.shape[0] // 2
    scaled = gram[...] / node_total

    def groups(block):
        return [block[TILE * g : TILE * (g + 1)] for g in range(half // TILE)]

    def rotated(values, factor):
        high = factor.astype(BF16).astype(F32)
        both = jnp.concatenate([high, factor - high], axis=0).astype(BF16)
        image = lax.dot_general(values, both, (NT, ((), ())), preferred_element_type=F32)
        return (image[:, :half] + image[:, half:]).astype(BF16)

    first = inverse_factor(groups(scaled[:half, :half]))
    below = full(scaled[half:, :half], first, NT)
    rest = scaled[half:, half:] - full(below, below, NT)
    load.wait()
    left = filtered[..., :half].reshape(-1, half)
    made[..., :half] = rotated(left, first).reshape(made.shape[:-1] + (half,))
    stores = [
        pltpu.make_async_copy(made.at[..., pl.ds(0, half)], out.at[..., pl.ds(0, half)], store_sem.at[0])
    ]
    stores[0].start()
    second = inverse_factor(groups(rest))
    corner = -full(second, full(below, first))
    bottom = jnp.concatenate([corner, second], axis=1)
    parts = 4
    step = made.shape[0] // parts
    for n in range(parts):
        block = filtered[n * step : (n + 1) * step]
        image = rotated(block.reshape(-1, block.shape[-1]), bottom)
        made[n * step : (n + 1) * step, :, :, half:] = image.reshape(block.shape[:-1] + (half,))
        where = (pl.ds(n * step, step), slice(None), slice(None), pl.ds(half, half))
        stores.append(pltpu.make_async_copy(made.at[where], out.at[where], store_sem.at[n + 1]))
        stores[-1].start()
    for store in stores:
        store.wait()


def rotate(node_total, gram, filtered):
    hbm = pl.BlockSpec(memory_space=pltpu.MemorySpace.HBM)
    return pl.pallas_call(
        functools.partial(rotate_kernel, node_total),
        out_shape=jax.ShapeDtypeStruct(filtered.shape, BF16),
        in_specs=[hbm] * 2,
        out_specs=hbm,
        scratch_shapes=[
            pltpu.VMEM(gram.shape, F32),
            pltpu.VMEM(filtered.shape, BF16),
            pltpu.VMEM(filtered.shape, BF16),
            pltpu.SemaphoreType.DMA((2,)),
            pltpu.SemaphoreType.DMA((5,)),
        ],
        compiler_params=pltpu.CompilerParams(vmem_limit_bytes=62 * 2**20),
    )(gram, filtered)


def local(sizes, orbitals, cell_block, potential):
    filtered, gram = filter_and_gram(sizes, orbitals, cell_block, potential)
    node_total = filtered.size // filtered.shape[-1] * sizes[0] * sizes[1] * sizes[2]
    return rotate(node_total, gram, filtered)


def solution(mesh):
    sizes = tuple(mesh.shape[name] for name in ("gx", "gy", "gz"))
    placed = (P("gx", "gy", "gz", None), P(), P("gx", "gy", "gz"))
    return jax.shard_map(
        functools.partial(local, sizes),
        mesh=mesh,
        in_specs=placed,
        out_specs=P("gx", "gy", "gz", None),
        check_vma=False,
    )
```

```python
import functools

import jax
import jax.numpy as jnp
import ml_dtypes
import numpy as np
from jax import lax
from jax.experimental import pallas as pl
from jax.experimental.pallas import tpu as pltpu
from jax.sharding import PartitionSpec as P

POLY = 8
SIDE = POLY + 1
CENTER = 6.0
HALF_WIDTH = 8.0
MESH = pl.DeviceIdType.MESH
F32 = jnp.float32
BF16 = jnp.bfloat16
HIGHEST = lax.Precision.HIGHEST
TILE = 8

COLS = SIDE * SIDE * POLY
ROWS = 736
PLANE = ROWS - COLS
LINE = SIDE * POLY

DIRECTIONS = sorted(
    [
        (dx, dy, dz)
        for dx in (-1, 0, 1)
        for dy in (-1, 0, 1)
        for dz in (-1, 0, 1)
        if (dx, dy, dz) != (0, 0, 0)
    ],
    key=lambda d: -sum(map(abs, d)),
)
LOW = [d for d in DIRECTIONS if max(d) <= 0]
HIGH = [d for d in DIRECTIONS if min(d) >= 0]


def column_rows(d):
    if d[2] != 0:
        return 0
    return 2 * LINE if 0 in d[:2] else 2 * POLY


def plane_rows(d):
    return 96 if d[:2] == (0, 0) else 16


OFFSET = {}
_at = 0
for _d in DIRECTIONS:
    OFFSET[_d] = _at
    _at += column_rows(_d) + plane_rows(_d)
MESSAGE_ROWS = _at


def message_rows(dirs):
    return sum(column_rows(d) + plane_rows(d) for d in dirs)


TOP = [d for d in DIRECTIONS if d[2] <= 0]
BOTTOM = [d for d in DIRECTIONS if d[2] > 0]


def edge_nodes(step):
    return [8] if step > 0 else [0] if step < 0 else list(range(SIDE))


def plane_nodes(d):
    return [(i, j) for i in edge_nodes(d[0]) for j in edge_nodes(d[1])]


def tables():
    order = np.zeros((ROWS, SIDE**3), np.float32)
    for i in range(SIDE):
        for j in range(SIDE):
            for k in range(POLY):
                order[i * LINE + j * POLY + k, i * 81 + j * 9 + k] = 1
            order[COLS + i * 9 + j, i * 81 + j * 9 + POLY] = 1
    pick = np.zeros((sum(plane_rows(d) for d in DIRECTIONS), ROWS), np.float32)
    at = 0
    for d in DIRECTIONS:
        for t, (i, j) in enumerate(plane_nodes(d)):
            pick[at + t, i * LINE + j * POLY if d[2] < 0 else COLS + i * 9 + j] = 1
        at += plane_rows(d)
    top = np.zeros((PLANE, sum(plane_rows(d) for d in TOP)), np.float32)
    at = 0
    for d in TOP:
        for t, (i, j) in enumerate(plane_nodes((-d[0], -d[1], 0))):
            top[i * 9 + j, at + t] = 1
        at += plane_rows(d)
    bottom = np.zeros((COLS, sum(plane_rows(d) for d in BOTTOM)), np.float32)
    at = 0
    for d in BOTTOM:
        for t, (i, j) in enumerate(plane_nodes((-d[0], -d[1], 0))):
            bottom[i * LINE + j * POLY, at + t] = 1
        at += plane_rows(d)
    insert = np.zeros((COLS, PLANE), np.float32)
    for i in range(SIDE):
        for j in range(SIDE):
            insert[i * LINE + j * POLY, i * 9 + j] = 1
    made = [order, pick, top, bottom, np.concatenate([insert, insert], 1), insert.T]
    return [m.astype(ml_dtypes.bfloat16) for m in made]


def dot(a, b):
    return jnp.dot(a, b, preferred_element_type=F32)


def filter_kernel(
    sizes,
    *refs,
):
    operands = refs[:9]
    filtered_out, gram_out = refs[9:11]
    held = refs[11:20]
    (
        load_sem, store_sem, filtered, operator, shift, sums, field0, field1, field2, send, recv, total, parts, planes, whole,
        send_sem, recv_sem, part_send_sem, part_recv_sem,
    ) = refs[20:]
    orbitals, potential, pick, cell, order, top, insert, extract, bottom = held
    nx, ny, nz = sizes
    me = (lax.axis_index("gx"), lax.axis_index("gy"), lax.axis_index("gz"))
    group = nx * ny
    mine = me[0] * ny + me[1]
    chunk = total.shape[0] // group

    def towards(d):
        return tuple(
            m if s == 0 else lax.rem(m + (s + n), n) for m, s, n in zip(me, d, sizes)
        )

    def member(t):
        x, y = lax.rem(me[0] + t // ny, nx), lax.rem(me[1] + t % ny, ny)
        return x * ny + y, (x, y, me[2])

    def distance(t):
        x, y = t // ny, t % ny
        return min(x, nx - x) + min(y, ny - y) / 2

    farthest_first = sorted(range(1, group), key=distance, reverse=True)
    layers_farthest_first = sorted(range(1, nz), key=lambda t: -min(t, nz - t))

    def above(t):
        return me[0], me[1], lax.rem(me[2] + t, nz)

    def tile(n):
        return pl.ds(pl.multiple_of(n * chunk, chunk), chunk)

    barrier = pltpu.get_barrier_semaphore()
    for d in HIGH:
        pl.semaphore_signal(barrier, inc=1, device_id=towards(d), device_id_type=MESH)

    loads = [
        pltpu.make_async_copy(operand, place, load_sem.at[n])
        for n, (operand, place) in enumerate(zip(operands, held))
    ]
    for load in loads:
        load.start()

    def column_slices(d):
        for c in range(2):
            if d[1] == 0:
                yield c, (0 if d[0] < 0 else 8) * LINE, LINE
            else:
                for i in edge_nodes(d[0]):
                    yield c, i * LINE + (0 if d[1] < 0 else 8) * POLY, POLY

    def pack(number, dirs):
        source = jnp.concatenate([sums[0, :COLS], sums[1, COLS:]], axis=0).astype(BF16)
        small = dot(pick[...], source).astype(BF16)
        at = 0
        for d in DIRECTIONS:
            columns, width = column_rows(d), plane_rows(d)
            if d in dirs:
                if columns:
                    pieces = [sums[c, r : r + w] for c, r, w in column_slices(d)]
                    send[number, pl.ds(OFFSET[d], columns)] = jnp.concatenate(
                        pieces, axis=0
                    ).astype(BF16)
                send[number, pl.ds(OFFSET[d] + columns, width)] = small[at : at + width]
            at += width

    def copies(number, dirs):
        for d in dirs:
            rows = pl.ds(OFFSET[d], column_rows(d) + plane_rows(d))
            yield pltpu.make_async_remote_copy(
                src_ref=send.at[number, rows],
                dst_ref=recv.at[number, rows],
                send_sem=send_sem.at[number],
                recv_sem=recv_sem.at[number],
                device_id=towards(d),
                device_id_type=MESH,
            )

    def finish(number, dirs, semaphore):
        arrived = recv.at[number, pl.ds(0, message_rows(dirs))]
        pltpu.make_async_copy(arrived, arrived, semaphore.at[number]).wait()

    def unpack(number, dirs):
        for d in dirs:
            if column_rows(d):
                got = recv[number, pl.ds(OFFSET[d], column_rows(d))].astype(F32)
                at = 0
                for c, r, w in column_slices((-d[0], -d[1], 0)):
                    sums[c, r : r + w] += got[at : at + w]
                    at += w

        def plane_parts(wanted):
            return jnp.concatenate(
                [
                    recv[number, pl.ds(OFFSET[d] + column_rows(d), plane_rows(d))]
                    if d in dirs
                    else jnp.zeros((plane_rows(d), recv.shape[-1]), BF16)
                    for d in wanted
                ],
                axis=0,
            )

        if dirs is not HIGH:
            sums[1, COLS:] += dot(top[...], plane_parts(TOP))
        if dirs is not LOW:
            sums[0, :COLS] += dot(bottom[...], plane_parts(BOTTOM))

    def exchange(number, dirs, meanwhile=None):
        pack(number, dirs)
        for copy in copies(number, dirs):
            copy.start()
        if meanwhile is not None:
            meanwhile()
        finish(number, dirs, recv_sem)
        unpack(number, dirs)

    def hold(field, first, second, last):
        closing = dot(extract[...], second.astype(BF16))
        field[0] = jnp.concatenate([first, closing], axis=0).astype(BF16)
        field[1] = jnp.concatenate([second, last], axis=0).astype(BF16)

    def apply_operator(field):
        for c in range(2):
            values = field[c]
            image = dot(operator[...], values)
            sums[c, :COLS] = image[:COLS] + shift[c] * values.astype(F32)[:COLS]
            sums[c, COLS:] = image[COLS:]
        plane = sums[0, COLS:]
        high = plane.astype(BF16).astype(F32)
        split = jnp.concatenate([high, plane - high], axis=0).astype(BF16)
        sums[1, :COLS] += dot(insert[...], split)

    sums[...] = jnp.zeros_like(sums)
    loads[0].wait()
    for i in range(POLY):
        layer = orbitals[i].astype(F32).reshape(POLY, 2, POLY, -1)
        for c in range(2):
            sums[c, i * LINE : i * LINE + 64] = layer[:, c].reshape(64, -1)

    def make_operator():
        loads[1].wait()
        shift[...] = jnp.zeros_like(shift)
        for i in range(POLY):
            scale = jnp.broadcast_to(
                (potential[i] - CENTER)[:, :, None], (POLY, 2 * POLY, shift.shape[-1])
            ).reshape(POLY, 2, POLY, -1)
            for c in range(2):
                shift[c, i * LINE : i * LINE + 64] = scale[:, c].reshape(64, -1)
        for load in loads[3:]:
            load.wait()
        turned = dot(order[...], cell[...]).astype(BF16)
        operator[...] = lax.dot_general(
            turned, order[...], (((1,), (1,)), ((), ())), preferred_element_type=F32
        ).astype(BF16)

    loads[2].wait()
    pl.semaphore_wait(barrier, len(LOW))
    exchange(0, LOW, make_operator)
    hold(field0, sums[0, :COLS], sums[1, :COLS], sums[1, COLS:])

    apply_operator(field0)
    exchange(1, DIRECTIONS)
    scaled = [sums[c] / HALF_WIDTH for c in range(2)]
    hold(field1, scaled[0][:COLS], scaled[1][:COLS], scaled[1][COLS:])

    apply_operator(field1)
    exchange(2, DIRECTIONS)
    scaled = [2.0 * sums[c] / HALF_WIDTH - field0[c].astype(F32) for c in range(2)]
    hold(field2, scaled[0][:COLS], scaled[1][:COLS], scaled[1][COLS:])

    apply_operator(field2)
    exchange(3, HIGH)
    for i in range(POLY):
        rows = slice(i * LINE, i * LINE + 64)
        halves = []
        for c in range(2):
            before = field1[c].astype(F32)[rows]
            now = 2.0 * sums[c, rows] / HALF_WIDTH - before
            halves.append(now.reshape(POLY, 1, POLY, -1))
        layer = jnp.concatenate(halves, axis=1).reshape(POLY, 2 * POLY, -1)
        filtered[i] = layer.astype(BF16)

    store = pltpu.make_async_copy(filtered, filtered_out, store_sem.at[0])
    store.start()
    flat = filtered[...].reshape(-1, filtered.shape[-1])
    total[...] = lax.dot_general(
        flat, flat, (((0,), (0,)), ((), ())), preferred_element_type=F32
    )

    def part_copy(phase, source, target, device):
        return pltpu.make_async_remote_copy(
            src_ref=source,
            dst_ref=target,
            send_sem=part_send_sem.at[phase],
            recv_sem=part_recv_sem.at[phase],
            device_id=device,
            device_id_type=MESH,
        )

    def part_wait(buffer, count, semaphore):
        some = buffer.at[pl.ds(0, count)]
        pltpu.make_async_copy(some, some, semaphore).wait()

    for t in farthest_first:
        other, device = member(t)
        part_copy(0, total.at[tile(other)], parts.at[mine], device).start()

    parts[mine] = total[tile(mine)]
    part_wait(parts, group - 1, part_recv_sem.at[0])
    planes[me[2]] = jnp.sum(parts[...], axis=0)

    for t in layers_farthest_first:
        part_copy(1, planes.at[me[2]], planes.at[me[2]], above(t)).start()

    part_wait(planes, nz - 1, part_recv_sem.at[1])
    whole[...] = jnp.sum(planes[...], axis=0)
    gram_store = pltpu.make_async_copy(whole, gram_out.at[tile(mine)], store_sem.at[1])

    for t in farthest_first:
        part_copy(2, whole, gram_out.at[tile(mine)], member(t)[1]).start()

    gram_store.start()
    part_wait(gram_out, (group - 1) * chunk, part_recv_sem.at[2])

    for number, dirs in enumerate((LOW, DIRECTIONS, DIRECTIONS, HIGH)):
        finish(number, dirs, send_sem)
    part_wait(parts, group - 1, part_send_sem.at[0])
    part_wait(planes, nz - 1, part_send_sem.at[1])
    part_wait(gram_out, (group - 1) * chunk, part_send_sem.at[2])
    store.wait()
    gram_store.wait()


def filter_and_gram(sizes, orbitals, cell_block, potential):
    width = orbitals.shape[-1]
    group = sizes[0] * sizes[1]
    order, pick, top, bottom, insert, extract = tables()
    operands = [orbitals, potential, pick, cell_block, order, top, insert, extract, bottom]
    hbm = pl.BlockSpec(memory_space=pltpu.MemorySpace.HBM)
    return pl.pallas_call(
        functools.partial(filter_kernel, sizes),
        out_shape=[
            jax.ShapeDtypeStruct(orbitals.shape, BF16),
            jax.ShapeDtypeStruct((width, width), F32),
        ],
        in_specs=[hbm] * len(operands),
        out_specs=[hbm] * 2,
        scratch_shapes=[pltpu.VMEM(a.shape, a.dtype) for a in operands]
        + [
            pltpu.SemaphoreType.DMA((len(operands),)),
            pltpu.SemaphoreType.DMA((2,)),
            pltpu.VMEM(orbitals.shape, BF16),
            pltpu.VMEM((ROWS, ROWS), BF16),
            pltpu.VMEM((2, COLS, width), F32),
            pltpu.VMEM((2, ROWS, width), F32),
            pltpu.VMEM((2, ROWS, width), BF16),
            pltpu.VMEM((2, ROWS, width), BF16),
            pltpu.VMEM((2, ROWS, width), BF16),
            pltpu.VMEM((4, MESSAGE_ROWS, width), BF16),
            pltpu.VMEM((4, MESSAGE_ROWS, width), BF16),
            pltpu.VMEM((width, width), F32),
            pltpu.VMEM((group, width // group, width), F32),
            pltpu.VMEM((sizes[2], width // group, width), F32),
            pltpu.VMEM((width // group, width), F32),
            pltpu.SemaphoreType.DMA((4,)),
            pltpu.SemaphoreType.DMA((4,)),
            pltpu.SemaphoreType.DMA((3,)),
            pltpu.SemaphoreType.DMA((3,)),
        ],
        compiler_params=pltpu.CompilerParams(
            collective_id=0, has_side_effects=True, vmem_limit_bytes=62 * 2**20
        ),
    )(*operands)


def spread_lane(x, n):
    return jnp.broadcast_to(x[:, n : n + 1], x.shape)


def spread_row(x, n):
    return jnp.broadcast_to(x[n : n + 1], x.shape)


def inverse_factor(rows):
    count = len(rows)
    shape = rows[0].shape
    height = lax.broadcasted_iota(jnp.int32, shape, 0)
    lane = lax.broadcasted_iota(jnp.int32, shape, 1)
    rows = list(rows)
    made = [jnp.where(lane == height + TILE * g, 1.0, 0.0).astype(F32) for g in range(count)]
    for b in range(count):
        lead, image = rows[b], made[b]
        columns = [spread_lane(lead, TILE * b + t) for t in range(TILE)]
        recips, coefs, lead_rows, image_rows = [], [], [], []
        pivots = jnp.ones(shape, F32)
        for t in range(TILE):
            pivot = spread_row(columns[t], t)
            recips.append(1.0 / pivot)
            pivots = jnp.where(height == t, pivot, pivots)
            factor = jnp.where(height > t, columns[t] * recips[t], 0.0)
            coefs.append({u: spread_row(columns[u], t) for u in range(t + 1, TILE)})
            for u in range(t + 1, TILE):
                columns[u] = columns[u] - factor * coefs[t][u]
            lead_rows.append(spread_row(lead, t))
            image_rows.append(spread_row(image, t))
            lead = lead - factor * lead_rows[t]
            image = image - factor * image_rows[t]
        made[b] = image * lax.rsqrt(pivots)
        for g in range(b + 1, count):
            entries = [spread_lane(rows[g], TILE * b + t) for t in range(TILE)]
            for t in range(TILE):
                factor = entries[t] * recips[t]
                for u in range(t + 1, TILE):
                    entries[u] = entries[u] - factor * coefs[t][u]
                rows[g] = rows[g] - factor * lead_rows[t]
                made[g] = made[g] - factor * image_rows[t]
    return jnp.concatenate(made, axis=0)


def full(a, b, contract=((1,), (0,))):
    return lax.dot_general(a, b, (contract, ((), ())), precision=HIGHEST, preferred_element_type=F32)


NT = ((1,), (1,))


def rotate_kernel(node_total, gram_in, filtered_in, out, gram, filtered, made, load_sem, store_sem):
    gram_load = pltpu.make_async_copy(gram_in, gram, load_sem.at[0])
    gram_load.start()
    load = pltpu.make_async_copy(filtered_in, filtered, load_sem.at[1])
    load.start()
    gram_load.wait()
    half = gram.shape[0] // 2
    scaled = gram[...] / node_total

    def groups(block):
        return [block[TILE * g : TILE * (g + 1)] for g in range(half // TILE)]

    def halves(x):
        high = x.astype(BF16)
        return high, (x - high.astype(F32)).astype(BF16)

    def product(values, factor):
        both = jnp.concatenate(halves(factor), axis=0)
        image = lax.dot_general(values, both, (NT, ((), ())), preferred_element_type=F32)
        return image[:, :half] + image[:, half:]

    first = inverse_factor(groups(scaled[:half, :half]))
    below = full(scaled[half:, :half], first, NT)
    rest = scaled[half:, half:] - full(below, below, NT)
    load.wait()
    left = filtered[..., :half].reshape(-1, half)
    made[..., :half] = product(left, first).astype(BF16).reshape(made.shape[:-1] + (half,))
    stores = [
        pltpu.make_async_copy(made.at[..., pl.ds(0, half)], out.at[..., pl.ds(0, half)], store_sem.at[0])
    ]
    stores[0].start()
    right = filtered[..., half:].reshape(-1, half).astype(F32)
    right_high, right_low = halves(right - product(left, full(below, first)))
    second_high, second_low = halves(inverse_factor(groups(rest)))
    factor = jnp.concatenate([second_high, second_low, second_high], axis=1)
    parts = 4
    step = made.shape[0] // parts
    height = left.shape[0] // parts
    for n in range(parts):
        rows = slice(n * height, (n + 1) * height)
        values = jnp.concatenate([right_high[rows], right_high[rows], right_low[rows]], axis=1)
        image = lax.dot_general(values, factor, (NT, ((), ())), preferred_element_type=F32)
        made[n * step : (n + 1) * step, :, :, half:] = image.astype(BF16).reshape(
            (step,) + made.shape[1:-1] + (half,)
        )
        where = (pl.ds(n * step, step), slice(None), slice(None), pl.ds(half, half))
        stores.append(pltpu.make_async_copy(made.at[where], out.at[where], store_sem.at[n + 1]))
        stores[-1].start()
    for store in stores:
        store.wait()


def rotate(node_total, gram, filtered):
    hbm = pl.BlockSpec(memory_space=pltpu.MemorySpace.HBM)
    return pl.pallas_call(
        functools.partial(rotate_kernel, node_total),
        out_shape=jax.ShapeDtypeStruct(filtered.shape, BF16),
        in_specs=[hbm] * 2,
        out_specs=hbm,
        scratch_shapes=[
            pltpu.VMEM(gram.shape, F32),
            pltpu.VMEM(filtered.shape, BF16),
            pltpu.VMEM(filtered.shape, BF16),
            pltpu.SemaphoreType.DMA((2,)),
            pltpu.SemaphoreType.DMA((5,)),
        ],
        compiler_params=pltpu.CompilerParams(vmem_limit_bytes=62 * 2**20),
    )(gram, filtered)


def local(sizes, orbitals, cell_block, potential):
    filtered, gram = filter_and_gram(sizes, orbitals, cell_block, potential)
    node_total = filtered.size // filtered.shape[-1] * sizes[0] * sizes[1] * sizes[2]
    return rotate(node_total, gram, filtered)


def solution(mesh):
    sizes = tuple(mesh.shape[name] for name in ("gx", "gy", "gz"))
    placed = (P("gx", "gy", "gz", None), P(), P("gx", "gy", "gz"))
    return jax.shard_map(
        functools.partial(local, sizes),
        mesh=mesh,
        in_specs=placed,
        out_specs=P("gx", "gy", "gz", None),
        check_vma=False,
    )
```

```python
import functools

import jax
import jax.numpy as jnp
import ml_dtypes
import numpy as np
from jax import lax
from jax.experimental import pallas as pl
from jax.experimental.pallas import tpu as pltpu
from jax.sharding import PartitionSpec as P

POLY = 8
SIDE = POLY + 1
CENTER = 6.0
HALF_WIDTH = 8.0
MESH = pl.DeviceIdType.MESH
F32 = jnp.float32
BF16 = jnp.bfloat16
HIGHEST = lax.Precision.HIGHEST
TILE = 8

COLS = SIDE * SIDE * POLY
ROWS = 736
PLANE = ROWS - COLS
LINE = SIDE * POLY

DIRECTIONS = sorted(
    [
        (dx, dy, dz)
        for dx in (-1, 0, 1)
        for dy in (-1, 0, 1)
        for dz in (-1, 0, 1)
        if (dx, dy, dz) != (0, 0, 0)
    ],
    key=lambda d: -sum(map(abs, d)),
)
LOW = [d for d in DIRECTIONS if max(d) <= 0]
HIGH = [d for d in DIRECTIONS if min(d) >= 0]


def column_rows(d):
    if d[2] != 0:
        return 0
    return 2 * LINE if 0 in d[:2] else 2 * POLY


def plane_rows(d):
    return 96 if d[:2] == (0, 0) else 16


OFFSET = {}
_at = 0
for _d in DIRECTIONS:
    OFFSET[_d] = _at
    _at += column_rows(_d) + plane_rows(_d)
MESSAGE_ROWS = _at


def message_rows(dirs):
    return sum(column_rows(d) + plane_rows(d) for d in dirs)


TOP = [d for d in DIRECTIONS if d[2] <= 0]
BOTTOM = [d for d in DIRECTIONS if d[2] > 0]


def edge_nodes(step):
    return [8] if step > 0 else [0] if step < 0 else list(range(SIDE))


def plane_nodes(d):
    return [(i, j) for i in edge_nodes(d[0]) for j in edge_nodes(d[1])]


def tables():
    order = np.zeros((ROWS, SIDE**3), np.float32)
    for i in range(SIDE):
        for j in range(SIDE):
            for k in range(POLY):
                order[i * LINE + j * POLY + k, i * 81 + j * 9 + k] = 1
            order[COLS + i * 9 + j, i * 81 + j * 9 + POLY] = 1
    pick = np.zeros((sum(plane_rows(d) for d in DIRECTIONS), ROWS), np.float32)
    at = 0
    for d in DIRECTIONS:
        for t, (i, j) in enumerate(plane_nodes(d)):
            pick[at + t, i * LINE + j * POLY if d[2] < 0 else COLS + i * 9 + j] = 1
        at += plane_rows(d)
    top = np.zeros((PLANE, sum(plane_rows(d) for d in TOP)), np.float32)
    at = 0
    for d in TOP:
        for t, (i, j) in enumerate(plane_nodes((-d[0], -d[1], 0))):
            top[i * 9 + j, at + t] = 1
        at += plane_rows(d)
    bottom = np.zeros((COLS, sum(plane_rows(d) for d in BOTTOM)), np.float32)
    at = 0
    for d in BOTTOM:
        for t, (i, j) in enumerate(plane_nodes((-d[0], -d[1], 0))):
            bottom[i * LINE + j * POLY, at + t] = 1
        at += plane_rows(d)
    insert = np.zeros((COLS, PLANE), np.float32)
    for i in range(SIDE):
        for j in range(SIDE):
            insert[i * LINE + j * POLY, i * 9 + j] = 1
    made = [order, pick, top, bottom, np.concatenate([insert, insert], 1), insert.T]
    return [m.astype(ml_dtypes.bfloat16) for m in made]


def dot(a, b):
    return jnp.dot(a, b, preferred_element_type=F32)


def filter_kernel(
    sizes,
    *refs,
):
    operands = refs[:9]
    filtered_out, gram_out = refs[9:11]
    held = refs[11:20]
    (
        load_sem, store_sem, filtered, operator, shift, sums, field0, field1, field2, send, recv, total, parts, planes, whole,
        send_sem, recv_sem, plane_sem, part_send_sem, part_recv_sem,
    ) = refs[20:]
    orbitals, potential, pick, cell, order, top, insert, extract, bottom = held
    nx, ny, nz = sizes
    me = (lax.axis_index("gx"), lax.axis_index("gy"), lax.axis_index("gz"))
    group = nx * ny
    mine = me[0] * ny + me[1]
    chunk = total.shape[0] // group

    def towards(d):
        return tuple(
            m if s == 0 else lax.rem(m + (s + n), n) for m, s, n in zip(me, d, sizes)
        )

    def member(t):
        x, y = lax.rem(me[0] + t // ny, nx), lax.rem(me[1] + t % ny, ny)
        return x * ny + y, (x, y, me[2])

    def distance(t):
        x, y = t // ny, t % ny
        return min(x, nx - x) + min(y, ny - y) / 2

    farthest_first = sorted(range(1, group), key=distance, reverse=True)
    layers_farthest_first = sorted(range(1, nz), key=lambda t: -min(t, nz - t))

    def above(t):
        return me[0], me[1], lax.rem(me[2] + t, nz)

    def tile(n):
        return pl.ds(pl.multiple_of(n * chunk, chunk), chunk)

    barrier = pltpu.get_barrier_semaphore()
    for d in HIGH:
        pl.semaphore_signal(barrier, inc=1, device_id=towards(d), device_id_type=MESH)

    loads = [
        pltpu.make_async_copy(operand, place, load_sem.at[n])
        for n, (operand, place) in enumerate(zip(operands, held))
    ]
    for load in loads:
        load.start()

    def column_slices(d):
        for c in range(2):
            if d[1] == 0:
                yield c, (0 if d[0] < 0 else 8) * LINE, LINE
            else:
                for i in edge_nodes(d[0]):
                    yield c, i * LINE + (0 if d[1] < 0 else 8) * POLY, POLY

    def pack(number, dirs):
        source = jnp.concatenate([sums[0, :COLS], sums[1, COLS:]], axis=0).astype(BF16)
        small = dot(pick[...], source).astype(BF16)
        at = 0
        for d in DIRECTIONS:
            columns, width = column_rows(d), plane_rows(d)
            if d in dirs:
                if columns:
                    pieces = [sums[c, r : r + w] for c, r, w in column_slices(d)]
                    send[number, pl.ds(OFFSET[d], columns)] = jnp.concatenate(
                        pieces, axis=0
                    ).astype(BF16)
                send[number, pl.ds(OFFSET[d] + columns, width)] = small[at : at + width]
            at += width

    def copies(number, dirs):
        for d in dirs:
            rows = pl.ds(OFFSET[d], column_rows(d) + plane_rows(d))
            yield pltpu.make_async_remote_copy(
                src_ref=send.at[number, rows],
                dst_ref=recv.at[number, rows],
                send_sem=send_sem.at[number],
                recv_sem=(plane_sem if d[2] else recv_sem).at[number],
                device_id=towards(d),
                device_id_type=MESH,
            )

    def finish(number, dirs, semaphore):
        arrived = recv.at[number, pl.ds(0, message_rows(dirs))]
        pltpu.make_async_copy(arrived, arrived, semaphore.at[number]).wait()

    def unpack(number, dirs):
        finish(number, [d for d in dirs if d[2] == 0], recv_sem)
        for d in dirs:
            if column_rows(d):
                got = recv[number, pl.ds(OFFSET[d], column_rows(d))].astype(F32)
                at = 0
                for c, r, w in column_slices((-d[0], -d[1], 0)):
                    sums[c, r : r + w] += got[at : at + w]
                    at += w

        finish(number, [d for d in dirs if d[2] != 0], plane_sem)

        def plane_parts(wanted):
            return jnp.concatenate(
                [
                    recv[number, pl.ds(OFFSET[d] + column_rows(d), plane_rows(d))]
                    if d in dirs
                    else jnp.zeros((plane_rows(d), recv.shape[-1]), BF16)
                    for d in wanted
                ],
                axis=0,
            )

        if dirs is not HIGH:
            sums[1, COLS:] += dot(top[...], plane_parts(TOP))
        if dirs is not LOW:
            sums[0, :COLS] += dot(bottom[...], plane_parts(BOTTOM))

    def exchange(number, dirs, meanwhile=None):
        pack(number, dirs)
        for copy in copies(number, dirs):
            copy.start()
        if meanwhile is not None:
            meanwhile()
        unpack(number, dirs)

    def hold(field, first, second, last):
        closing = dot(extract[...], second.astype(BF16))
        field[0] = jnp.concatenate([first, closing], axis=0).astype(BF16)
        field[1] = jnp.concatenate([second, last], axis=0).astype(BF16)

    def apply_operator(field):
        for c in (1, 0):
            values = field[c]
            image = dot(operator[...], values)
            sums[c, :COLS] = image[:COLS] + shift[c] * values.astype(F32)[:COLS]
            sums[c, COLS:] = image[COLS:]
        plane = sums[0, COLS:]
        high = plane.astype(BF16).astype(F32)
        split = jnp.concatenate([high, plane - high], axis=0).astype(BF16)
        sums[1, :COLS] += dot(insert[...], split)

    sums[...] = jnp.zeros_like(sums)
    loads[0].wait()
    for i in range(POLY):
        layer = orbitals[i].astype(F32).reshape(POLY, 2, POLY, -1)
        for c in range(2):
            sums[c, i * LINE : i * LINE + 64] = layer[:, c].reshape(64, -1)

    def make_operator():
        loads[1].wait()
        shift[...] = jnp.zeros_like(shift)
        for i in range(POLY):
            scale = jnp.broadcast_to(
                (potential[i] - CENTER)[:, :, None], (POLY, 2 * POLY, shift.shape[-1])
            ).reshape(POLY, 2, POLY, -1)
            for c in range(2):
                shift[c, i * LINE : i * LINE + 64] = scale[:, c].reshape(64, -1)
        for load in loads[3:]:
            load.wait()
        turned = dot(order[...], cell[...]).astype(BF16)
        operator[...] = lax.dot_general(
            turned, order[...], (((1,), (1,)), ((), ())), preferred_element_type=F32
        ).astype(BF16)

    loads[2].wait()
    pl.semaphore_wait(barrier, len(LOW))
    exchange(0, LOW, make_operator)
    hold(field0, sums[0, :COLS], sums[1, :COLS], sums[1, COLS:])

    apply_operator(field0)
    exchange(1, DIRECTIONS)
    scaled = [sums[c] / HALF_WIDTH for c in range(2)]
    hold(field1, scaled[0][:COLS], scaled[1][:COLS], scaled[1][COLS:])

    apply_operator(field1)
    exchange(2, DIRECTIONS)
    scaled = [2.0 * sums[c] / HALF_WIDTH - field0[c].astype(F32) for c in range(2)]
    hold(field2, scaled[0][:COLS], scaled[1][:COLS], scaled[1][COLS:])

    apply_operator(field2)
    exchange(3, HIGH)
    for i in range(POLY):
        rows = slice(i * LINE, i * LINE + 64)
        halves = []
        for c in range(2):
            before = field1[c].astype(F32)[rows]
            now = 2.0 * sums[c, rows] / HALF_WIDTH - before
            halves.append(now.reshape(POLY, 1, POLY, -1))
        layer = jnp.concatenate(halves, axis=1).reshape(POLY, 2 * POLY, -1)
        filtered[i] = layer.astype(BF16)

    store = pltpu.make_async_copy(filtered, filtered_out, store_sem.at[0])
    store.start()
    flat = filtered[...].reshape(-1, filtered.shape[-1])
    total[...] = lax.dot_general(
        flat, flat, (((0,), (0,)), ((), ())), preferred_element_type=F32
    )

    def part_copy(phase, source, target, device):
        return pltpu.make_async_remote_copy(
            src_ref=source,
            dst_ref=target,
            send_sem=part_send_sem.at[phase],
            recv_sem=part_recv_sem.at[phase],
            device_id=device,
            device_id_type=MESH,
        )

    def part_wait(buffer, count, semaphore):
        some = buffer.at[pl.ds(0, count)]
        pltpu.make_async_copy(some, some, semaphore).wait()

    for t in farthest_first:
        other, device = member(t)
        part_copy(0, total.at[tile(other)], parts.at[mine], device).start()

    parts[mine] = total[tile(mine)]
    part_wait(parts, group - 1, part_recv_sem.at[0])
    planes[me[2]] = jnp.sum(parts[...], axis=0)

    for t in layers_farthest_first:
        part_copy(1, planes.at[me[2]], planes.at[me[2]], above(t)).start()

    part_wait(planes, nz - 1, part_recv_sem.at[1])
    whole[...] = jnp.sum(planes[...], axis=0)
    gram_store = pltpu.make_async_copy(whole, gram_out.at[tile(mine)], store_sem.at[1])

    for t in farthest_first:
        part_copy(2, whole, gram_out.at[tile(mine)], member(t)[1]).start()

    gram_store.start()
    part_wait(gram_out, (group - 1) * chunk, part_recv_sem.at[2])

    for number, dirs in enumerate((LOW, DIRECTIONS, DIRECTIONS, HIGH)):
        finish(number, dirs, send_sem)
    part_wait(parts, group - 1, part_send_sem.at[0])
    part_wait(planes, nz - 1, part_send_sem.at[1])
    part_wait(gram_out, (group - 1) * chunk, part_send_sem.at[2])
    store.wait()
    gram_store.wait()


def filter_and_gram(sizes, orbitals, cell_block, potential):
    width = orbitals.shape[-1]
    group = sizes[0] * sizes[1]
    order, pick, top, bottom, insert, extract = tables()
    operands = [orbitals, potential, pick, cell_block, order, top, insert, extract, bottom]
    hbm = pl.BlockSpec(memory_space=pltpu.MemorySpace.HBM)
    return pl.pallas_call(
        functools.partial(filter_kernel, sizes),
        out_shape=[
            jax.ShapeDtypeStruct(orbitals.shape, BF16),
            jax.ShapeDtypeStruct((width, width), F32),
        ],
        in_specs=[hbm] * len(operands),
        out_specs=[hbm] * 2,
        scratch_shapes=[pltpu.VMEM(a.shape, a.dtype) for a in operands]
        + [
            pltpu.SemaphoreType.DMA((len(operands),)),
            pltpu.SemaphoreType.DMA((2,)),
            pltpu.VMEM(orbitals.shape, BF16),
            pltpu.VMEM((ROWS, ROWS), BF16),
            pltpu.VMEM((2, COLS, width), F32),
            pltpu.VMEM((2, ROWS, width), F32),
            pltpu.VMEM((2, ROWS, width), BF16),
            pltpu.VMEM((2, ROWS, width), BF16),
            pltpu.VMEM((2, ROWS, width), BF16),
            pltpu.VMEM((4, MESSAGE_ROWS, width), BF16),
            pltpu.VMEM((4, MESSAGE_ROWS, width), BF16),
            pltpu.VMEM((width, width), F32),
            pltpu.VMEM((group, width // group, width), F32),
            pltpu.VMEM((sizes[2], width // group, width), F32),
            pltpu.VMEM((width // group, width), F32),
            pltpu.SemaphoreType.DMA((4,)),
            pltpu.SemaphoreType.DMA((4,)),
            pltpu.SemaphoreType.DMA((4,)),
            pltpu.SemaphoreType.DMA((3,)),
            pltpu.SemaphoreType.DMA((3,)),
        ],
        compiler_params=pltpu.CompilerParams(
            collective_id=0, has_side_effects=True, vmem_limit_bytes=62 * 2**20
        ),
    )(*operands)


def spread_lane(x, n):
    return jnp.broadcast_to(x[:, n : n + 1], x.shape)


def spread_row(x, n):
    return jnp.broadcast_to(x[n : n + 1], x.shape)


def inverse_factor(rows):
    count = len(rows)
    shape = rows[0].shape
    height = lax.broadcasted_iota(jnp.int32, shape, 0)
    lane = lax.broadcasted_iota(jnp.int32, shape, 1)
    rows = list(rows)
    made = [jnp.where(lane == height + TILE * g, 1.0, 0.0).astype(F32) for g in range(count)]
    for b in range(count):
        lead, image = rows[b], made[b]
        columns = [spread_lane(lead, TILE * b + t) for t in range(TILE)]
        recips, coefs, lead_rows, image_rows = [], [], [], []
        pivots = jnp.ones(shape, F32)
        for t in range(TILE):
            pivot = spread_row(columns[t], t)
            recips.append(1.0 / pivot)
            pivots = jnp.where(height == t, pivot, pivots)
            factor = jnp.where(height > t, columns[t] * recips[t], 0.0)
            coefs.append({u: spread_row(columns[u], t) for u in range(t + 1, TILE)})
            for u in range(t + 1, TILE):
                columns[u] = columns[u] - factor * coefs[t][u]
            lead_rows.append(spread_row(lead, t))
            image_rows.append(spread_row(image, t))
            lead = lead - factor * lead_rows[t]
            image = image - factor * image_rows[t]
        made[b] = image * lax.rsqrt(pivots)
        for g in range(b + 1, count):
            entries = [spread_lane(rows[g], TILE * b + t) for t in range(TILE)]
            for t in range(TILE):
                factor = entries[t] * recips[t]
                for u in range(t + 1, TILE):
                    entries[u] = entries[u] - factor * coefs[t][u]
                rows[g] = rows[g] - factor * lead_rows[t]
                made[g] = made[g] - factor * image_rows[t]
    return jnp.concatenate(made, axis=0)


def full(a, b, contract=((1,), (0,))):
    return lax.dot_general(a, b, (contract, ((), ())), precision=HIGHEST, preferred_element_type=F32)


NT = ((1,), (1,))


def rotate_kernel(node_total, gram_in, filtered_in, out, gram, filtered, made, load_sem, store_sem):
    gram_load = pltpu.make_async_copy(gram_in, gram, load_sem.at[0])
    gram_load.start()
    load = pltpu.make_async_copy(filtered_in, filtered, load_sem.at[1])
    load.start()
    gram_load.wait()
    half = gram.shape[0] // 2
    scaled = gram[...] / node_total

    def groups(block):
        return [block[TILE * g : TILE * (g + 1)] for g in range(half // TILE)]

    def halves(x):
        high = x.astype(BF16)
        return high, (x - high.astype(F32)).astype(BF16)

    def product(values, factor):
        both = jnp.concatenate(halves(factor), axis=0)
        image = lax.dot_general(values, both, (NT, ((), ())), preferred_element_type=F32)
        return image[:, :half] + image[:, half:]

    first = inverse_factor(groups(scaled[:half, :half]))
    below = full(scaled[half:, :half], first, NT)
    rest = scaled[half:, half:] - full(below, below, NT)
    load.wait()
    left = filtered[..., :half].reshape(-1, half)
    made[..., :half] = product(left, first).astype(BF16).reshape(made.shape[:-1] + (half,))
    stores = [
        pltpu.make_async_copy(made.at[..., pl.ds(0, half)], out.at[..., pl.ds(0, half)], store_sem.at[0])
    ]
    stores[0].start()
    right = filtered[..., half:].reshape(-1, half).astype(F32)
    right_high, right_low = halves(right - product(left, full(below, first)))
    second_high, second_low = halves(inverse_factor(groups(rest)))
    factor = jnp.concatenate([second_high, second_low, second_high], axis=1)
    parts = 4
    step = made.shape[0] // parts
    height = left.shape[0] // parts
    for n in range(parts):
        rows = slice(n * height, (n + 1) * height)
        values = jnp.concatenate([right_high[rows], right_high[rows], right_low[rows]], axis=1)
        image = lax.dot_general(values, factor, (NT, ((), ())), preferred_element_type=F32)
        made[n * step : (n + 1) * step, :, :, half:] = image.astype(BF16).reshape(
            (step,) + made.shape[1:-1] + (half,)
        )
        where = (pl.ds(n * step, step), slice(None), slice(None), pl.ds(half, half))
        stores.append(pltpu.make_async_copy(made.at[where], out.at[where], store_sem.at[n + 1]))
        stores[-1].start()
    for store in stores:
        store.wait()


def rotate(node_total, gram, filtered):
    hbm = pl.BlockSpec(memory_space=pltpu.MemorySpace.HBM)
    return pl.pallas_call(
        functools.partial(rotate_kernel, node_total),
        out_shape=jax.ShapeDtypeStruct(filtered.shape, BF16),
        in_specs=[hbm] * 2,
        out_specs=hbm,
        scratch_shapes=[
            pltpu.VMEM(gram.shape, F32),
            pltpu.VMEM(filtered.shape, BF16),
            pltpu.VMEM(filtered.shape, BF16),
            pltpu.SemaphoreType.DMA((2,)),
            pltpu.SemaphoreType.DMA((5,)),
        ],
        compiler_params=pltpu.CompilerParams(vmem_limit_bytes=62 * 2**20),
    )(gram, filtered)


def local(sizes, orbitals, cell_block, potential):
    filtered, gram = filter_and_gram(sizes, orbitals, cell_block, potential)
    node_total = filtered.size // filtered.shape[-1] * sizes[0] * sizes[1] * sizes[2]
    return rotate(node_total, gram, filtered)


def solution(mesh):
    sizes = tuple(mesh.shape[name] for name in ("gx", "gy", "gz"))
    placed = (P("gx", "gy", "gz", None), P(), P("gx", "gy", "gz"))
    return jax.shard_map(
        functools.partial(local, sizes),
        mesh=mesh,
        in_specs=placed,
        out_specs=P("gx", "gy", "gz", None),
        check_vma=False,
    )
```
